1024 devices in a mesh: dp: 16 (over z_hi, x, core), expert: 64 (over z_lo, y).
Axes of the slice: x: 4, y: 4, z: 32 (z_hi: 2, z_lo: 16; z = z_hi * 16 + z_lo), core: 2. Of those that a mesh axis runs over, the one named last changes fastest.
Arguments:
- out_grad: bfloat16 [2, 1024, 4096], P(None, 'expert', 'dp'), may hold values from -6 to 6
- expert_ids: int32 [2, 1024, 8], P(None, 'expert'), may hold values from 0 to 63, all different within a row; in each aligned block of 16 rows (0 to 15, 16 to 31, ..., all dimensions but the last counted through in order) at most 4 rows name the same one
- probs: bfloat16 [2, 1024, 8], P(None, 'expert'), may hold values from 0.019897461 to 0.5
- saved_inputs: bfloat16 [2, 64, 256, 4096], P(None, 'expert', None, 'dp'), may hold values from -6 to 6
- gate_pre: bfloat16 [2, 64, 256, 768], P(None, 'expert'), may hold values from -6 to 6
- up_pre: bfloat16 [2, 64, 256, 768], P(None, 'expert'), may hold values from -6 to 6
- w_gate: bfloat16 [64, 4096, 768], P('expert', 'dp'), may hold values from -0.09375 to 0.09375
- w_up: bfloat16 [64, 4096, 768], P('expert', 'dp'), may hold values from -0.09375 to 0.09375
- w_down: bfloat16 [64, 768, 4096], P('expert', None, 'dp'), may hold values from -0.21875 to 0.21875
Outputs:
- in_grad: bfloat16 [2, 1024, 4096], P(None, 'expert', 'dp')
- prob_grad: bfloat16 [2, 1024, 8], P(None, 'expert')
- grad_gate: bfloat16 [64, 4096, 768], P('expert', 'dp')
- grad_up: bfloat16 [64, 4096, 768], P('expert', 'dp')
- grad_down: bfloat16 [64, 768, 4096], P('expert', None, 'dp')
The draws below stay inside these ranges and needn't reach their ends.
Inputs may be any that keep to these rules, and one draw needn't show every extreme that they name: `expert_ids`: in each microbatch, the routes of the 16 tokens of one index of expert name any expert at most 4 times, a bound that some block reaches.
All inputs are finite; a program needn't handle non-finite values.
Results may differ from the reference program's by a relative error of at most 0.0057.
Values may be sent and summed in bfloat16 or wider, within the bound.
No kernel may reach another device: no remote copies, remote signals or barrier semaphores. Data moves between devices by JAX's collectives and lax.ppermute only.
A program may use at most 32 MiB of HBM per device.

```python
import math
import jax
import jax.numpy as jnp
import numpy as np
from jax import lax

D = 4096
FF = 768
TOP = 8
MB = 2
TOK_DEV = 16
EXPERTS = 64
CAP = 4
SLOTS = 256
TOKENS = 1024
N_EXPERT = 64


def block_levels(own_key, extent, shards, low, top_value):
    def one(dim, blocks):
        heights = jax.random.uniform(jax.random.fold_in(jax.random.fold_in(own_key, 6), dim), (blocks,), jnp.float32, low / len(shards), top_value / len(shards))
        return jnp.repeat(jnp.exp(heights), extent[dim] // blocks).reshape((-1,) + (1,) * (len(extent) - dim - 1))

    factor_of = one(*shards[0])
    for cut in shards[1:]:
        factor_of = factor_of * one(*cut)
    return factor_of


def assign_block(own_key, own, number, rows, amount, top, most, lean):
    ranking = jax.random.permutation(own_key, amount)
    heavy_load, common = portions_of(amount, rows * top, most, lean, True), portions_of(amount, rows * top, most, lean, False)
    places = jnp.arange(amount)

    def named(lengths, offset_by):
        used = int((lengths > 0).sum())
        fixed = max(1, used // 4)
        moved = fixed + (places - fixed + offset_by * (used - fixed)) % max(1, amount - fixed)
        return jnp.zeros((amount,), jnp.int32).at[ranking[jnp.where(places < fixed, places, moved)]].set(jnp.asarray(lengths, jnp.int32))

    lengths = jnp.where(number % 4 == 0, named(heavy_load, number // 4), named(common, number - number // 4 - 1))
    mixed = jax.random.permutation(jax.random.fold_in(own, 3), amount)
    source_of, sink = mixed[0:amount // 2 * 2:2], mixed[1:amount // 2 * 2:2]
    room = jnp.minimum(lengths[source_of] - 1, most - lengths[sink]) // 2
    room = jnp.where((source_of == ranking[0]) | (sink == ranking[0]) | (lengths[sink] == 0), 0, jnp.maximum(room, 0))
    moved = jax.random.randint(jax.random.fold_in(own, 4), (amount // 2,), 0, 1 << 20) % (room + 1)
    lengths = lengths.at[source_of].add(-moved).at[sink].add(moved)
    items = jnp.searchsorted(jnp.cumsum(lengths), jnp.arange(rows * top), side="right").astype(jnp.int32)
    table = items.reshape(top, rows).T
    table = table[jax.random.permutation(jax.random.fold_in(own, 1), rows)]
    offset_by = jax.random.randint(jax.random.fold_in(own, 2), (rows, 1), 0, top)
    return jnp.take_along_axis(table, (jnp.arange(top)[None, :] + offset_by) % top, axis=1)


def portions_of(amount, total, reach, lean, full):
    portions = [(1 << 20) // math.isqrt(rank ** lean) + 1 for rank in range(1, amount + 1)]
    largest = reach if full else min(reach, max(-(-total // amount), total * portions[0] // sum(portions)))
    least = 1 if total - largest >= amount - 1 else 0
    given, surplus = [largest] + [least] * (amount - 1), total - largest - least * (amount - 1)
    while surplus > 0:
        free = [i for i in range(1, amount) if given[i] < largest] or [i for i in range(1, amount) if given[i] < reach]
        pool, remaining = sum([portions[i] for i in free]), surplus
        for i in free:
            extra = min(reach - given[i], max(1, remaining * portions[i] // pool), surplus)
            given[i] = given[i] + extra
            surplus = surplus - extra
    return np.array(given)


def centred(stream_key, shape, deviation, limit, shards=(), held_as=jnp.bfloat16):
    level = block_levels(stream_key, shape, shards, -0.22, 0.18) if shards else 1.0
    entries = jax.random.normal(stream_key, shape, jnp.float32) * deviation * level
    return jnp.minimum(jnp.maximum(entries, -limit), limit).astype(held_as)


def setup_inputs(seed: int = 0) -> dict:
    seeds = jax.random.split(jax.random.key(seed), 10)
    out_grad = centred(seeds[0], (MB, TOKENS, D), 1.0, 6.0, ((1, 64), (2, 16)))
    expert_ids_keys = jax.random.split(jax.random.fold_in(seeds[1], 1), MB * TOKENS // TOK_DEV)
    expert_ids_turns = jax.random.permutation(jax.random.fold_in(seeds[1], 3), MB * TOKENS // TOK_DEV)
    expert_ids = jax.vmap(lambda own, number: assign_block(jax.random.fold_in(seeds[1], 2), own, number, TOK_DEV, EXPERTS, TOP, CAP, 2))(expert_ids_keys, expert_ids_turns).reshape((MB, TOKENS, TOP))
    probs = jnp.clip(jnp.exp(math.log(0.5) - 3.224016 * jax.random.uniform(seeds[2], (MB, TOKENS, TOP), jnp.float32) ** block_levels(seeds[2], (MB, TOKENS, TOP), ((1, 64),), -0.2, 0.2)), 0.019897461, 0.5).astype(jnp.bfloat16)
    saved_inputs = centred(seeds[3], (MB, EXPERTS, SLOTS, D), 1.0, 6.0, ((1, 64), (3, 16)))
    gate_pre = centred(seeds[4], (MB, EXPERTS, SLOTS, FF), 1.5, 6.0, ((1, 64),))
    up_pre = centred(seeds[5], (MB, EXPERTS, SLOTS, FF), 1.0, 6.0, ((1, 64),))
    w_gate = centred(seeds[6], (EXPERTS, D, FF), D ** -0.5, 0.09375, ((0, 64), (1, 16)))
    w_up = centred(seeds[7], (EXPERTS, D, FF), D ** -0.5, 0.09375, ((0, 64), (1, 16)))
    w_down = centred(seeds[8], (EXPERTS, FF, D), FF ** -0.5, 0.21875, ((0, 64), (2, 16)))
    return {"out_grad": out_grad, "expert_ids": expert_ids, "probs": probs, "saved_inputs": saved_inputs, "gate_pre": gate_pre, "up_pre": up_pre, "w_gate": w_gate, "w_up": w_up, "w_down": w_down}


def silu_parts(gate_f):
    sig = jax.nn.sigmoid(gate_f)
    return gate_f * sig, sig * (1.0 + gate_f * (1.0 - sig))


def contract(left, right, left_dim, right_dim):
    return lax.dot_general(left, right, (((left_dim,), (right_dim,)), ((), ())), preferred_element_type=jnp.float32)


def reference(out_grad, expert_ids, probs, saved_inputs, gate_pre, up_pre, w_gate, w_up, w_down):
    routes = TOK_DEV * TOP
    ids = expert_ids.reshape(MB, N_EXPERT, routes)
    hits = (ids[..., None] == jnp.arange(EXPERTS, dtype=jnp.int32)).astype(jnp.int32)
    earlier = jnp.cumsum(hits, axis=2) - hits
    slot = jnp.sum(earlier * hits, axis=3).astype(jnp.int32)
    row = (jnp.arange(N_EXPERT, dtype=jnp.int32)[None, :, None] * CAP + slot).reshape(MB, TOKENS * TOP)
    expert = expert_ids.reshape(MB, TOKENS * TOP)
    token = jnp.arange(TOKENS * TOP, dtype=jnp.int32) // TOP
    grads_in = []
    probs_in = []
    for m in range(MB):
        grads_in.append(jnp.zeros((EXPERTS, SLOTS, D), jnp.bfloat16).at[expert[m], row[m]].set(out_grad[m][token]))
        probs_in.append(jnp.zeros((EXPERTS, SLOTS), jnp.bfloat16).at[expert[m], row[m]].set(probs[m].reshape(-1)))
    grads_in = jnp.stack(grads_in, 1)
    probs_in = jnp.stack(probs_in, 1)

    def one_expert(items):
        rows, weights, inputs, gates, ups, wg, wu, wd = items
        acc_gate = jnp.zeros((D, FF), jnp.float32)
        acc_up = jnp.zeros((D, FF), jnp.float32)
        acc_down = jnp.zeros((FF, D), jnp.float32)
        slot_rows = []
        slot_probs = []
        for m in range(MB):
            gate_f = gates[m].astype(jnp.float32)
            up_f = ups[m].astype(jnp.float32)
            act, slope = silu_parts(gate_f)
            hidden = act * up_f
            weight_f = weights[m].astype(jnp.float32)[:, None]
            summed = contract(rows[m], wd, 1, 1)
            slot_probs.append(jnp.sum(summed * hidden, axis=1).astype(jnp.bfloat16))
            dh = weight_f * summed
            dgate = (dh * up_f * slope).astype(jnp.bfloat16)
            dup = (dh * act).astype(jnp.bfloat16)
            scaled = (weight_f * hidden).astype(jnp.bfloat16)
            acc_down = acc_down + contract(scaled, rows[m], 0, 0)
            acc_gate = acc_gate + contract(inputs[m], dgate, 0, 0)
            acc_up = acc_up + contract(inputs[m], dup, 0, 0)
            slot_rows.append((contract(dgate, wg, 1, 1) + contract(dup, wu, 1, 1)).astype(jnp.bfloat16))
        return (jnp.stack(slot_rows, 0), jnp.stack(slot_probs, 0), acc_gate.astype(jnp.bfloat16),
                acc_up.astype(jnp.bfloat16), acc_down.astype(jnp.bfloat16))

    items = (grads_in, probs_in, saved_inputs.transpose(1, 0, 2, 3), gate_pre.transpose(1, 0, 2, 3),
             up_pre.transpose(1, 0, 2, 3), w_gate, w_up, w_down)
    slot_grad, slot_prob, grad_gate, grad_up, grad_down = lax.map(one_expert, items)
    in_grads = []
    prob_grads = []
    for m in range(MB):
        picked = slot_grad[expert[m], m, row[m]].astype(jnp.float32).reshape(TOKENS, TOP, D)
        in_grads.append(jnp.sum(picked, axis=1).astype(jnp.bfloat16))
        prob_grads.append(slot_prob[expert[m], m, row[m]].reshape(TOKENS, TOP))
    return jnp.stack(in_grads, 0), jnp.stack(prob_grads, 0), grad_gate, grad_up, grad_down
```

```python
import jax
import jax.numpy as jnp
from jax import lax
from jax.sharding import Mesh
from jax.sharding import PartitionSpec as P

BF = jnp.bfloat16
F32 = jnp.float32
DP = ("zh", "x", "core")
EX = ("zl", "y")


def dot(a, b, ca, cb):
    return lax.dot_general(a, b, (((ca,), (cb,)), ((), ())), preferred_element_type=F32)


def silu_parts(g):
    sig = jax.nn.sigmoid(g)
    return g * sig, sig * (1.0 + g * (1.0 - sig))


def route_maps(ids_m, n_expert, cap):
    toks, top = ids_m.shape
    flat = ids_m.reshape(-1)
    hits = (flat[:, None] == jnp.arange(n_expert, dtype=jnp.int32)[None, :]).astype(jnp.int32)
    earlier = jnp.cumsum(hits, axis=0) - hits
    slot = jnp.sum(earlier * hits, axis=1)
    dest = slot * n_expert + flat
    placed = jnp.arange(n_expert * cap, dtype=jnp.int32)[:, None] == dest[None, :]
    token_map = jnp.sum(placed.reshape(n_expert * cap, toks, top).astype(jnp.int32), axis=2)
    return placed, token_map.astype(BF)


def local(out_grad, expert_ids, probs, saved_inputs, gate_pre, up_pre, w_gate, w_up, w_down):
    ne = lax.axis_size(EX)
    mb, toks, top = expert_ids.shape
    slots = saved_inputs.shape[2]
    cap = slots // ne
    width = out_grad.shape[2]
    ff = w_gate.shape[2]
    pad = 128
    line = cap * width + pad

    placed, tmap = zip(*[route_maps(expert_ids[m], ne, cap) for m in range(mb)])
    send = []
    for m in range(mb):
        rows = dot(tmap[m], out_grad[m], 1, 0).astype(BF)
        wts = jnp.sum(jnp.where(placed[m], probs[m].reshape(1, -1).astype(F32), 0.0), axis=1)
        wts = jnp.pad(wts.astype(BF).reshape(cap, ne).T, ((0, 0), (0, pad - cap)))
        parts = [rows[s * ne : (s + 1) * ne] for s in range(cap)] + [wts]
        send.append(jnp.concatenate(parts, axis=1))
    got = lax.all_to_all(jnp.stack(send, 1), EX, 0, 0, tiled=True)

    g = [got[:, m, : cap * width].reshape(slots, width) for m in range(mb)]
    p = [got[:, m, cap * width : cap * width + cap].reshape(slots).astype(F32) for m in range(mb)]
    g_all = jnp.concatenate(g, 0)
    p_all = jnp.concatenate(p, 0)

    part = dot(g_all, w_down[0], 1, 1)
    n_c, n_x = lax.axis_size("core"), lax.axis_size("x")
    r = part.shape[0]
    r_c = r // n_c
    r_x = r_c // n_x
    me_c, me_x = lax.axis_index("core"), lax.axis_index("x")
    t = lax.all_to_all(part.astype(BF).reshape(n_c, r_c, ff), "core", 0, 0, tiled=True)
    half = jnp.sum(t.astype(F32), axis=0)
    t = lax.all_to_all(half.astype(BF).reshape(n_x, r_x, ff), "x", 0, 0, tiled=True)
    eighth = jnp.sum(t.astype(F32), axis=0).astype(BF)
    other = lax.ppermute(eighth, "zh", [(0, 1), (1, 0)])
    u = eighth.astype(F32) + other.astype(F32)

    start = me_c * r_c + me_x * r_x
    gate_all = gate_pre[:, 0].reshape(r, ff)
    up_all = up_pre[:, 0].reshape(r, ff)
    gate_f = lax.dynamic_slice_in_dim(gate_all, start, r_x, 0).astype(F32)
    up_f = lax.dynamic_slice_in_dim(up_all, start, r_x, 0).astype(F32)
    w_f = lax.dynamic_slice_in_dim(p_all, start, r_x, 0)[:, None]
    act, slope = silu_parts(gate_f)
    slot_prob = jnp.sum(u * (act * up_f), axis=1, keepdims=True).astype(BF)
    dh = w_f * u
    dgate = (dh * up_f * slope).astype(BF)
    dup = (dh * act).astype(BF)
    mine = jnp.concatenate([dgate, dup, jnp.pad(slot_prob, ((0, 0), (0, pad - 1)))], axis=1)
    mine = jnp.broadcast_to(mine[None], (n_x,) + mine.shape)
    full = lax.all_to_all(mine, "x", 0, 0, tiled=True).reshape(r_c, -1)
    full = lax.all_gather(full, "core", axis=0, tiled=True)
    dgate, dup = full[:, :ff], full[:, ff : 2 * ff]
    slot_prob = full[:, 2 * ff]

    slot_rows = (dot(dgate, w_gate[0], 1, 1) + dot(dup, w_up[0], 1, 1)).astype(BF)
    back = []
    for m in range(mb):
        rows = slot_rows[m * slots : (m + 1) * slots].reshape(ne, cap * width)
        sp = slot_prob[m * slots : (m + 1) * slots].reshape(ne, cap)
        back.append(jnp.concatenate([rows, jnp.pad(sp, ((0, 0), (0, pad - cap)))], axis=1))
    home = lax.all_to_all(jnp.stack(back, 1), EX, 0, 0, tiled=True)

    x_all = saved_inputs[:, 0].reshape(r, width)
    grad_gate = dot(x_all, dgate, 0, 0).astype(BF)
    grad_up = dot(x_all, dup, 0, 0).astype(BF)
    gate_f = gate_all.astype(F32)
    hidden = gate_f * jax.nn.sigmoid(gate_f) * up_all.astype(F32)
    scaled = (p_all[:, None] * hidden).astype(BF)
    grad_down = dot(scaled, g_all, 0, 0).astype(BF)

    in_grad, prob_grad = [], []
    for m in range(mb):
        rows = jnp.concatenate(
            [home[:, m, s * width : (s + 1) * width] for s in range(cap)], axis=0
        )
        in_grad.append(dot(tmap[m], rows, 0, 0).astype(BF))
        sp = home[:, m, cap * width : cap * width + cap].T.reshape(-1, 1).astype(F32)
        prob_grad.append(
            jnp.sum(jnp.where(placed[m], sp, 0.0), axis=0).astype(BF).reshape(toks, top)
        )
    return (
        jnp.stack(in_grad, 0),
        jnp.stack(prob_grad, 0),
        grad_gate[None],
        grad_up[None],
        grad_down[None],
    )


def solution(mesh):
    n_dp, n_ex = mesh.devices.shape
    fine = Mesh(
        mesh.devices.reshape(2, n_dp // 4, 2, n_ex // 4, 4), ("zh", "x", "core", "zl", "y")
    )
    specs = (
        P(None, EX, DP),
        P(None, EX, None),
        P(None, EX, None),
        P(None, EX, None, DP),
        P(None, EX, None, None),
        P(None, EX, None, None),
        P(EX, DP, None),
        P(EX, DP, None),
        P(EX, None, DP),
    )
    return jax.shard_map(
        local,
        mesh=fine,
        in_specs=specs,
        out_specs=(specs[0], specs[1], specs[6], specs[7], specs[8]),
        check_vma=False,
    )
```

```python
import jax
import jax.numpy as jnp
from jax import lax
from jax.sharding import Mesh
from jax.sharding import PartitionSpec as P

BF = jnp.bfloat16
F32 = jnp.float32
DP = ("zh", "x", "core")
EX = ("zl", "y")


def dot(a, b, ca, cb):
    return lax.dot_general(a, b, (((ca,), (cb,)), ((), ())), preferred_element_type=F32)


def silu_parts(g):
    sig = jax.nn.sigmoid(g)
    return g * sig, sig * (1.0 + g * (1.0 - sig))


def route_maps(ids_m, n_expert, cap):
    toks, top = ids_m.shape
    experts = jnp.arange(n_expert, dtype=jnp.int32)
    picks = (ids_m[:, :, None] == experts).astype(F32)
    hits = jnp.sum(picks, axis=1)
    earlier = jnp.tril(jnp.ones((toks, toks), F32), -1)
    slot = dot(earlier.astype(BF), hits.astype(BF), 1, 0)
    maps = [(hits * (slot == s)).astype(BF) for s in range(cap)]
    return picks, maps


def local(out_grad, expert_ids, probs, saved_inputs, gate_pre, up_pre, w_gate, w_up, w_down):
    ne = lax.axis_size(EX)
    mb, toks, top = expert_ids.shape
    slots = saved_inputs.shape[2]
    cap = slots // ne
    width = out_grad.shape[2]
    ff = w_gate.shape[2]
    pad = 128
    me_c = lax.axis_index("core")

    def turn(v):
        return jnp.where(me_c == 0, v, v[::-1])

    out_grad, expert_ids, probs = turn(out_grad), turn(expert_ids), turn(probs)
    saved_inputs, gate_pre, up_pre = turn(saved_inputs), turn(gate_pre), turn(up_pre)
    line = cap * width + pad

    picks, maps = zip(*[route_maps(expert_ids[m], ne, cap) for m in range(mb)])
    columns = jnp.arange(pad)
    send = []
    for m in range(mb):
        rows = [dot(k, out_grad[m], 0, 0).astype(BF) for k in maps[m]]
        prob = jnp.sum(picks[m] * probs[m].astype(F32)[:, :, None], axis=1).astype(BF)
        wts = sum(
            dot(k * prob, jnp.broadcast_to((columns == s).astype(BF), (toks, pad)), 0, 0)
            for s, k in enumerate(maps[m])
        )
        send.append(jnp.concatenate(rows + [wts.astype(BF)], axis=1))
    got = lax.all_to_all(jnp.stack(send, 1), EX, 0, 0, tiled=True)

    g = [got[:, m, : cap * width].reshape(slots, width) for m in range(mb)]
    p = [got[:, m, cap * width : cap * width + cap].reshape(slots).astype(F32) for m in range(mb)]
    g_all = jnp.concatenate(g, 0)
    p_all = jnp.concatenate(p, 0)

    n_x = lax.axis_size("x")
    r_x = slots // n_x
    swap = [(0, 1), (1, 0)]
    away = lax.ppermute(dot(g[1], w_down[0], 1, 1), "core", swap)
    half = dot(g[0], w_down[0], 1, 1) + away
    t = lax.all_to_all(half.astype(BF).reshape(n_x, r_x, ff), "x", 0, 0, tiled=True)
    eighth = jnp.sum(t.astype(F32), axis=0).astype(BF)
    other = lax.ppermute(eighth, "zh", swap)
    u = (eighth.astype(F32) + other.astype(F32)).astype(BF)
    u = jnp.broadcast_to(u[None], (n_x,) + u.shape)
    u_mine = lax.all_to_all(u, "x", 0, 0, tiled=True).reshape(slots, ff)
    u_all = [u_mine, lax.ppermute(u_mine, "core", swap)]

    dgates, dups, back = [], [], []
    for m in range(mb):
        gate_f = gate_pre[m, 0].astype(F32)
        up_f = up_pre[m, 0].astype(F32)
        act, slope = silu_parts(gate_f)
        u = u_all[m].astype(F32)
        slot_prob = jnp.sum(u * (act * up_f), axis=1).astype(BF)
        dh = p[m][:, None] * u
        dgate = (dh * up_f * slope).astype(BF)
        dup = (dh * act).astype(BF)
        rows = (dot(dgate, w_gate[0], 1, 1) + dot(dup, w_up[0], 1, 1)).astype(BF)
        sp = jnp.pad(slot_prob.reshape(ne, cap), ((0, 0), (0, pad - cap)))
        back.append(jnp.concatenate([rows.reshape(ne, cap * width), sp], axis=1))
        dgates.append(dgate)
        dups.append(dup)
    dgate = jnp.concatenate(dgates, 0)
    dup = jnp.concatenate(dups, 0)
    home = lax.all_to_all(jnp.stack(back, 1), EX, 0, 0, tiled=True)

    r = mb * slots
    x_all = saved_inputs[:, 0].reshape(r, width)
    grad_gate = dot(x_all, dgate, 0, 0).astype(BF)
    grad_up = dot(x_all, dup, 0, 0).astype(BF)
    gate_f = gate_pre[:, 0].reshape(r, ff).astype(F32)
    hidden = gate_f * jax.nn.sigmoid(gate_f) * up_pre[:, 0].reshape(r, ff).astype(F32)
    scaled = (p_all[:, None] * hidden).astype(BF)
    grad_down = dot(scaled, g_all, 0, 0).astype(BF)

    in_grad, prob_grad = [], []
    for m in range(mb):
        grads = sum(
            dot(k, home[:, m, s * width : (s + 1) * width], 1, 0) for s, k in enumerate(maps[m])
        )
        in_grad.append(grads.astype(BF))
        sp = home[:, m, cap * width : cap * width + cap].astype(F32)
        sp = sum(k.astype(F32) * sp[None, :, s] for s, k in enumerate(maps[m]))
        prob_grad.append(jnp.sum(picks[m] * sp[:, None, :], axis=2).astype(BF))
    return (
        turn(jnp.stack(in_grad, 0)),
        turn(jnp.stack(prob_grad, 0)),
        grad_gate[None],
        grad_up[None],
        grad_down[None],
    )


def solution(mesh):
    n_dp, n_ex = mesh.devices.shape
    fine = Mesh(
        mesh.devices.reshape(2, n_dp // 4, 2, n_ex // 4, 4), ("zh", "x", "core", "zl", "y")
    )
    specs = (
        P(None, EX, DP),
        P(None, EX, None),
        P(None, EX, None),
        P(None, EX, None, DP),
        P(None, EX, None, None),
        P(None, EX, None, None),
        P(EX, DP, None),
        P(EX, DP, None),
        P(EX, None, DP),
    )
    return jax.shard_map(
        local,
        mesh=fine,
        in_specs=specs,
        out_specs=(specs[0], specs[1], specs[6], specs[7], specs[8]),
        check_vma=False,
    )
```

```python
import functools

import jax
import jax.numpy as jnp
from jax import lax
from jax.experimental import pallas as pl
from jax.experimental.pallas import tpu as pltpu
from jax.sharding import Mesh
from jax.sharding import PartitionSpec as P

BF = jnp.bfloat16
F32 = jnp.float32
DP = ("zh", "x", "core")
EX = ("zl", "y")
PAD = 128
SWAP = [(0, 1), (1, 0)]
VMEM = pl.BlockSpec(memory_space=pltpu.VMEM)
SMEM = pl.BlockSpec(memory_space=pltpu.SMEM)


def dot(a, b, ca, cb):
    return lax.dot_general(a, b, (((ca,), (cb,)), ((), ())), preferred_element_type=F32)


def iota(shape, dim):
    return lax.broadcasted_iota(jnp.int32, shape, dim)


def call(body, outs, n_in, flops, bytes_moved, limit=24, has_me=True):
    first = [SMEM] if has_me else []
    return pl.pallas_call(
        body,
        out_shape=outs,
        in_specs=first + [VMEM] * n_in,
        out_specs=[VMEM] * len(outs),
        cost_estimate=pl.CostEstimate(flops=flops, bytes_accessed=bytes_moved, transcendentals=0),
        compiler_params=pltpu.CompilerParams(vmem_limit_bytes=limit << 20),
    )


def route_maps(ids, ne, cap):
    toks, top = ids.shape
    experts = iota((toks, ne), 1)
    picks = [(ids[:, k : k + 1] == experts).astype(F32) for k in range(top)]
    hits = functools.reduce(jnp.add, picks)
    lower = (iota((toks, toks), 0) > iota((toks, toks), 1)).astype(F32)
    slot = dot(lower.astype(BF), hits.astype(BF), 1, 0)
    maps = [jnp.where(slot == s, hits, 0.0) for s in range(cap)]
    return picks, maps


def pack_kernel(ne, cap, me, ids, probs, rows, out):
    mb, toks, width = rows.shape
    line = cap * width + PAD
    for m in range(mb):
        at = me[0] ^ m
        picks, maps = route_maps(ids[at], ne, cap)
        prob = probs[at].astype(F32)
        held = functools.reduce(
            jnp.add, [k * prob[:, i : i + 1] for i, k in enumerate(picks)]
        )
        tail = jnp.zeros((ne, PAD), F32)
        grads = rows[at]
        for s, k in enumerate(maps):
            base = m * line + s * width
            out[:, base : base + width] = dot(k.astype(BF), grads, 0, 0).astype(BF)
            column = (iota((toks, PAD), 1) == s).astype(BF)
            tail = tail + dot((k * held).astype(BF), column, 0, 0)
        base = m * line + cap * width
        out[:, base : base + PAD] = tail.astype(BF)


def spread(ne, cap, s):
    shape = (ne * cap, ne)
    return (iota(shape, 0) == iota(shape, 1) * cap + s).astype(BF)


def down_kernel(ne, cap, m, got, w_down, part, rows, probs):
    width = rows.shape[1]
    base = m * (cap * width + PAD)
    total = jnp.zeros(rows.shape, F32)
    for s in range(cap):
        total = total + dot(
            spread(ne, cap, s), got[:, base + s * width : base + (s + 1) * width], 1, 0
        )
    mine = total.astype(BF)
    rows[...] = mine
    part[...] = dot(mine, w_down[...], 1, 1)
    shape = (ne * cap, ne)
    source = iota(shape, 0)
    repeat = ((source >= iota(shape, 1) * cap) & (source < (iota(shape, 1) + 1) * cap)).astype(BF)
    tail = dot(repeat, got[:, base + cap * width : base + cap * width + PAD], 1, 0)
    shape = (ne * cap, PAD)
    probs[...] = jnp.sum(
        jnp.where(iota(shape, 1) == lax.rem(iota(shape, 0), cap), tail, 0.0), axis=1, keepdims=True
    )


def act_kernel(me, gate, up, probs0, probs1, rows0, rows1, f_gate, f_up, hidden, grad):
    total = None
    for m, (probs, rows) in enumerate(((probs0, rows0), (probs1, rows1))):
        gate_f = gate[me[0] ^ m].astype(F32)
        up_f = up[me[0] ^ m].astype(F32)
        p = probs[...]
        sig = 1.0 / (1.0 + jnp.exp(-gate_f))
        act = gate_f * sig
        h = act * up_f
        f_gate[m] = p * up_f * (sig * (1.0 + gate_f * (1.0 - sig)))
        f_up[m] = p * act
        hidden[m] = h
        term = dot((p * h).astype(BF), rows[...], 0, 0)
        total = term if total is None else total + term
    grad[...] = total.astype(BF)


def slot_kernel(ne, cap, m, u_ref, f_gate, f_up, hidden, w_gate, w_up, dgate, dup, out):
    u = u_ref[...].astype(F32)
    dg = (u * f_gate[m]).astype(BF)
    du = (u * f_up[m]).astype(BF)
    dgate[...] = dg
    dup[...] = du
    rows = (dot(dg, w_gate[...], 1, 1) + dot(du, w_up[...], 1, 1)).astype(BF)
    width = rows.shape[1]
    for s in range(cap):
        out[:, s * width : (s + 1) * width] = dot(spread(ne, cap, s), rows, 0, 0).astype(BF)
    slot_prob = jnp.sum(u * hidden[m], axis=1, keepdims=True)
    shape = (ne * cap, PAD)
    tail = jnp.where(iota(shape, 1) == lax.rem(iota(shape, 0), cap), slot_prob, 0.0).astype(BF)
    shape = (ne, ne * cap)
    slot = iota(shape, 1)
    gather = ((slot >= iota(shape, 0) * cap) & (slot < (iota(shape, 0) + 1) * cap)).astype(BF)
    out[:, cap * width :] = dot(gather, tail, 1, 0).astype(BF)


def weight_kernel(me, inputs, dgate0, dup0, dgate1, dup1, grad_gate, grad_up):
    first, second = inputs[me[0]], inputs[me[0] ^ 1]
    grad_gate[...] = (dot(first, dgate0[...], 0, 0) + dot(second, dgate1[...], 0, 0)).astype(BF)
    grad_up[...] = (dot(first, dup0[...], 0, 0) + dot(second, dup1[...], 0, 0)).astype(BF)


def unpack_kernel(ne, cap, me, ids, home, in_grad, prob_grad):
    mb, toks, width = in_grad.shape
    top = ids.shape[2]
    line = cap * width + PAD
    for m in range(mb):
        at = me[0] ^ m
        picks, maps = route_maps(ids[at], ne, cap)
        total = jnp.zeros((toks, width), F32)
        held = jnp.zeros((toks, ne), F32)
        tail = home[:, m * line + cap * width : (m + 1) * line]
        for s, k in enumerate(maps):
            base = m * line + s * width
            total = total + dot(k.astype(BF), home[:, base : base + width], 1, 0)
            column = (iota((toks, PAD), 1) == s).astype(BF)
            held = held + k * dot(column, tail, 1, 1)
        in_grad[at] = total.astype(BF)
        lane = iota((toks, top), 1)
        picked = jnp.zeros((toks, top), F32)
        for i, k in enumerate(picks):
            picked = jnp.where(lane == i, jnp.sum(k * held, axis=1, keepdims=True), picked)
        prob_grad[at] = picked.astype(BF)


def local(out_grad, expert_ids, probs, saved_inputs, gate_pre, up_pre, w_gate, w_up, w_down):
    sds = jax.ShapeDtypeStruct
    ne = lax.axis_size(EX)
    n_x = lax.axis_size("x")
    mb, toks, top = expert_ids.shape
    slots = saved_inputs.shape[2]
    cap = slots // ne
    width = out_grad.shape[2]
    ff = w_gate.shape[2]
    line = cap * width + PAD
    w_gate, w_up, w_down = w_gate[0], w_up[0], w_down[0]
    core = lax.axis_index("core")
    me = core.astype(jnp.int32).reshape(1)
    product = 2 * slots * width * ff

    send = call(
        functools.partial(pack_kernel, ne, cap),
        [sds((ne, mb * line), BF)],
        3,
        product // 8,
        ne * mb * line * 2,
    )(me, expert_ids, probs, out_grad)[0]
    got = lax.all_to_all(send.reshape(ne, mb, line), EX, 0, 0, tiled=True).reshape(ne, mb * line)

    def down(m):
        return call(
            functools.partial(down_kernel, ne, cap, m),
            [sds((slots, ff), F32), sds((slots, width), BF), sds((slots, 1), F32)],
            2,
            product,
            slots * ff * 4,
            has_me=False,
        )(got, w_down)

    part1, rows1, probs1 = down(1)
    away = lax.ppermute(part1, "core", SWAP)
    part0, rows0, probs0 = down(0)
    half = (part0 + away).astype(BF).reshape(n_x, slots // n_x, ff)
    half = lax.all_to_all(half, "x", 0, 0, tiled=True)
    eighth = jnp.sum(half.astype(F32), axis=0).astype(BF)
    both = lax.all_to_all(jnp.broadcast_to(eighth[None], (2,) + eighth.shape), "zh", 0, 0, tiled=True)

    f_gate, f_up, hidden, grad_down = call(
        act_kernel,
        [sds((mb, slots, ff), F32)] * 3 + [sds((ff, width), BF)],
        6,
        2 * product,
        mb * slots * ff * 16,
        limit=32,
    )(me, gate_pre[:, 0], up_pre[:, 0], probs0, probs1, rows0, rows1)

    u = jnp.sum(both.astype(F32), axis=0).astype(BF)
    u = jnp.broadcast_to(u[None], (n_x,) + u.shape)
    u0 = lax.all_to_all(u, "x", 0, 0, tiled=True).reshape(slots, ff)
    u1 = lax.ppermute(u0, "core", SWAP)

    def slot(m, u_m):
        return call(
            functools.partial(slot_kernel, ne, cap, m),
            [sds((slots, ff), BF), sds((slots, ff), BF), sds((ne, line), BF)],
            6,
            2 * product,
            slots * ff * 16,
            has_me=False,
        )(u_m, f_gate, f_up, hidden, w_gate, w_up)

    dgate0, dup0, back0 = slot(0, u0)
    dgate1, dup1, back1 = slot(1, u1)
    back = jnp.stack([back0, back1], axis=1)
    home = lax.all_to_all(back, EX, 0, 0, tiled=True).reshape(ne, mb * line)
    grad_gate, grad_up = call(
        weight_kernel, [sds((width, ff), BF)] * 2, 5, 4 * product, slots * ff * 12
    )(me, saved_inputs[:, 0], dgate0, dup0, dgate1, dup1)
    in_grad, prob_grad = call(
        functools.partial(unpack_kernel, ne, cap),
        [sds((mb, toks, width), BF), sds((mb, toks, top), BF)],
        2,
        product // 8,
        ne * mb * line * 2,
    )(me, expert_ids, home)
    return in_grad, prob_grad, grad_gate[None], grad_up[None], grad_down[None]


def solution(mesh):
    n_dp, n_ex = mesh.devices.shape
    fine = Mesh(
        mesh.devices.reshape(2, n_dp // 4, 2, n_ex // 4, 4), ("zh", "x", "core", "zl", "y")
    )
    specs = (
        P(None, EX, DP),
        P(None, EX, None),
        P(None, EX, None),
        P(None, EX, None, DP),
        P(None, EX, None, None),
        P(None, EX, None, None),
        P(EX, DP, None),
        P(EX, DP, None),
        P(EX, None, DP),
    )
    return jax.shard_map(
        local,
        mesh=fine,
        in_specs=specs,
        out_specs=(specs[0], specs[1], specs[6], specs[7], specs[8]),
        check_vma=False,
    )
```

```python
import functools

import jax
import jax.numpy as jnp
from jax import lax
from jax.experimental import pallas as pl
from jax.experimental.pallas import tpu as pltpu
from jax.sharding import Mesh
from jax.sharding import PartitionSpec as P

BF = jnp.bfloat16
F32 = jnp.float32
DP = ("zh", "x", "core")
EX = ("za", "zb", "y")
PLANE = ("zb", "y")
PAD = 128
SWAP = [(0, 1), (1, 0)]
VMEM = pl.BlockSpec(memory_space=pltpu.VMEM)
SMEM = pl.BlockSpec(memory_space=pltpu.SMEM)


def dot(a, b, ca, cb):
    return lax.dot_general(a, b, (((ca,), (cb,)), ((), ())), preferred_element_type=F32)


def iota(shape, dim):
    return lax.broadcasted_iota(jnp.int32, shape, dim)


def call(body, outs, n_in, flops, bytes_moved, limit=24, has_me=True):
    first = [SMEM] if has_me else []
    return pl.pallas_call(
        body,
        out_shape=outs,
        in_specs=first + [VMEM] * n_in,
        out_specs=[VMEM] * len(outs),
        cost_estimate=pl.CostEstimate(flops=flops, bytes_accessed=bytes_moved, transcendentals=0),
        compiler_params=pltpu.CompilerParams(vmem_limit_bytes=limit << 20),
    )


def flat_kernel(me, ids, probs, rows, out):
    mb, toks, width = rows.shape
    top = ids.shape[2]
    lane = iota((toks, PAD), 1)
    for m in range(mb):
        at = me[0] ^ m
        held = probs[at].astype(F32)
        names = ids[at].astype(F32)
        tail = jnp.zeros((toks, PAD), F32)
        for k in range(top):
            tail = jnp.where(lane == k, names[:, k : k + 1], tail)
            tail = jnp.where(lane == top + k, held[:, k : k + 1], tail)
        for peer in range(out.shape[0]):
            out[peer, m * toks : (m + 1) * toks, :width] = rows[at]
            out[peer, m * toks : (m + 1) * toks, width:] = tail.astype(BF)


def route_maps(names, first, size, nq, toks, cap):
    tokens, top = names.shape
    shape = (tokens, size)
    column = iota(shape, 1)
    expert = (first + lax.div(column, nq)).astype(F32)
    same = lax.div(iota(shape, 0), toks) == lax.rem(column, nq)
    picks = [jnp.where(same & (names[:, k : k + 1] == expert), 1.0, 0.0) for k in range(top)]
    hits = functools.reduce(jnp.add, picks)
    lower = jnp.where(iota((tokens, tokens), 0) > iota((tokens, tokens), 1), 1.0, 0.0)
    slot = dot(lower.astype(BF), hits.astype(BF), 1, 0)
    return picks, [jnp.where(slot == s, hits, 0.0) for s in range(cap)]


def pack_kernel(dims, first, lines, out):
    nd, nq, toks, top, cap, width = dims
    tail_in = lines[:, width:].astype(F32)
    picks, maps = route_maps(tail_in[:, :top], first[0], nd * nq, nq, toks, cap)
    grads = lines[:, :width]
    tokens = grads.shape[0]
    held = functools.reduce(
        jnp.add, [k * tail_in[:, top + i : top + i + 1] for i, k in enumerate(picks)]
    )
    tail = jnp.zeros((nd * nq, PAD), F32)
    for s, k in enumerate(maps):
        out[:, s * width : (s + 1) * width] = dot(k.astype(BF), grads, 0, 0).astype(BF)
        lane = jnp.where(iota((tokens, PAD), 1) == s, 1.0, 0.0).astype(BF)
        tail = tail + dot((k * held).astype(BF), lane, 0, 0)
    out[:, cap * width :] = tail.astype(BF)


def unpack_kernel(dims, first, lines, home, out):
    nd, nq, toks, top, cap, width = dims
    names = lines[:, width:].astype(F32)[:, :top]
    picks, maps = route_maps(names, first[0], nd * nq, nq, toks, cap)
    tokens = names.shape[0]
    total = jnp.zeros((tokens, width), F32)
    held = jnp.zeros((tokens, nd * nq), F32)
    tail = home[:, cap * width :]
    for s, k in enumerate(maps):
        total = total + dot(k.astype(BF), home[:, s * width : (s + 1) * width], 1, 0)
        lane = jnp.where(iota((tokens, PAD), 1) == s, 1.0, 0.0).astype(BF)
        held = held + k * dot(lane, tail, 1, 1)
    out[:, :width] = total.astype(BF)
    lane = iota((tokens, PAD), 1)
    picked = jnp.zeros((tokens, PAD), F32)
    for i, k in enumerate(picks):
        picked = jnp.where(lane == i, jnp.sum(k * held, axis=1, keepdims=True), picked)
    out[:, width:] = picked.astype(BF)


def total_kernel(me, parts, in_grad, prob_grad):
    mb, toks, width = in_grad.shape
    top = prob_grad.shape[2]
    for m in range(mb):
        total = functools.reduce(
            jnp.add,
            [
                parts[i, m * toks : (m + 1) * toks, :].astype(F32)
                for i in range(parts.shape[0])
            ],
        )
        in_grad[me[0] ^ m] = total[:, :width].astype(BF)
        prob_grad[me[0] ^ m] = total[:, width : width + top].astype(BF)


def first_row(shape, nd, nq, mb, cap):
    column = iota(shape, 1)
    return (lax.div(lax.rem(column, nq), mb) * nd + lax.div(column, nq)) * cap


def spread(nd, nq, mb, cap, m, s=None):
    rows = (nd * nq // mb) * cap
    shape = (rows, nd * nq)
    ahead = iota(shape, 0) - first_row(shape, nd, nq, mb, cap)
    here = (ahead >= 0) & (ahead < cap) if s is None else ahead == s
    here = here & (lax.rem(iota(shape, 1), mb) == m)
    return jnp.where(here, 1.0, 0.0).astype(BF)


def down_kernel(nd, nq, mb, cap, m, got, w_down, part, rows, probs):
    slots, width = rows.shape
    total = jnp.zeros((slots, width), F32)
    for s in range(cap):
        total = total + dot(
            spread(nd, nq, mb, cap, m, s), got[:, s * width : (s + 1) * width], 1, 0
        )
    mine = total.astype(BF)
    rows[...] = mine
    part[...] = dot(mine, w_down[...], 1, 1)
    tail = dot(spread(nd, nq, mb, cap, m), got[:, cap * width :], 1, 0)
    shape = (slots, PAD)
    probs[...] = jnp.sum(
        jnp.where(iota(shape, 1) == lax.rem(iota(shape, 0), cap), tail, 0.0), axis=1, keepdims=True
    )


def sum_kernel(mine, own, others, out):
    n = others.shape[0]
    total = functools.reduce(
        jnp.add, [jnp.where(mine[0] == i, own[i], others[i].astype(F32)) for i in range(n)]
    ).astype(BF)
    for i in range(out.shape[0]):
        out[i] = total


def pair_kernel(both, out):
    total = (both[0].astype(F32) + both[1].astype(F32)).astype(BF)
    for i in range(out.shape[0]):
        out[i] = total


def act_kernel(me, gate, up, probs0, probs1, rows0, rows1, f_gate, f_up, hidden, grad):
    total = None
    for m, (probs, rows) in enumerate(((probs0, rows0), (probs1, rows1))):
        gate_f = gate[me[0] ^ m].astype(F32)
        up_f = up[me[0] ^ m].astype(F32)
        p = probs[...]
        sig = 1.0 / (1.0 + jnp.exp(-gate_f))
        act = gate_f * sig
        h = act * up_f
        f_gate[m] = p * up_f * (sig * (1.0 + gate_f * (1.0 - sig)))
        f_up[m] = p * act
        hidden[m] = h
        term = dot((p * h).astype(BF), rows[...], 0, 0)
        total = term if total is None else total + term
    grad[...] = total.astype(BF)


def slot_kernel(nd, nq, mb, cap, m, u_ref, f_gate, f_up, hidden, w_gate, w_up, *rest):
    before, (dgate, dup, out) = rest[:-3], rest[-3:]
    u = u_ref[...].astype(F32)
    dg = (u * f_gate[m]).astype(BF)
    du = (u * f_up[m]).astype(BF)
    dgate[...] = dg
    dup[...] = du
    rows = (dot(dg, w_gate[...], 1, 1) + dot(du, w_up[...], 1, 1)).astype(BF)
    slots, width = rows.shape

    def put(low, high, value):
        if before:
            value = value + before[0][:, low:high].astype(F32)
        out[:, low:high] = value.astype(BF)

    for s in range(cap):
        put(s * width, (s + 1) * width, dot(spread(nd, nq, mb, cap, m, s), rows, 0, 0))
    slot_prob = jnp.sum(u * hidden[m], axis=1, keepdims=True)
    shape = (slots, PAD)
    tail = jnp.where(iota(shape, 1) == lax.rem(iota(shape, 0), cap), slot_prob, 0.0).astype(BF)
    put(cap * width, cap * width + PAD, dot(spread(nd, nq, mb, cap, m), tail, 0, 0))


def weight_kernel(me, inputs, dgate0, dup0, dgate1, dup1, grad_gate, grad_up):
    first, second = inputs[me[0]], inputs[me[0] ^ 1]
    grad_gate[...] = (dot(first, dgate0[...], 0, 0) + dot(second, dgate1[...], 0, 0)).astype(BF)
    grad_up[...] = (dot(first, dup0[...], 0, 0) + dot(second, dup1[...], 0, 0)).astype(BF)


def local(out_grad, expert_ids, probs, saved_inputs, gate_pre, up_pre, w_gate, w_up, w_down):
    sds = jax.ShapeDtypeStruct
    ne = lax.axis_size(EX)
    n_x = lax.axis_size("x")
    mb, toks, top = expert_ids.shape
    slots = saved_inputs.shape[2]
    cap = slots // ne
    width = out_grad.shape[2]
    ff = w_gate.shape[2]
    line = cap * width + PAD
    w_gate, w_up, w_down = w_gate[0], w_up[0], w_down[0]
    core = lax.axis_index("core")
    me = core.astype(jnp.int32).reshape(1)
    product = 2 * slots * width * ff

    n_a, nd = lax.axis_size("za"), lax.axis_size(PLANE)
    nq = n_a * mb
    dims = (nd, nq, toks, top, cap, width)
    first = (lax.axis_index("za").astype(jnp.int32) * nd).reshape(1)

    flat = call(flat_kernel, [sds((n_a, mb * toks, width + PAD), BF)], 3, 0, toks * width * 20)(
        me, expert_ids, probs, out_grad
    )[0]
    lines = lax.all_to_all(flat, "za", 0, 0, tiled=True).reshape(nq * toks, width + PAD)
    send = call(
        functools.partial(pack_kernel, dims), [sds((nd * nq, line), BF)], 1, product // 4, nd * nq * line * 2
    )(first, lines)[0]
    got = lax.all_to_all(send.reshape(nd, nq, line), PLANE, 0, 0, tiled=True).reshape(nd * nq, line)

    def down(m):
        return call(
            functools.partial(down_kernel, nd, nq, mb, cap, m),
            [sds((slots, ff), F32), sds((slots, width), BF), sds((slots, 1), F32)],
            2,
            product,
            slots * ff * 4,
            has_me=False,
        )(got, w_down)

    part1, rows1, probs1 = down(1)
    away = lax.ppermute(part1, "core", SWAP)
    part0, rows0, probs0 = down(0)
    half = (part0 + away).reshape(n_x, slots // n_x, ff)
    others = lax.all_to_all(half.astype(BF), "x", 0, 0, tiled=True)
    mine = lax.axis_index("x").astype(jnp.int32).reshape(1)
    piece = (slots // n_x, ff)
    eighth = call(
        sum_kernel, [sds((2,) + piece, BF)], 2, 0, slots * ff * 6
    )(mine, half, others)[0]
    both = lax.all_to_all(eighth, "zh", 0, 0, tiled=True)

    f_gate, f_up, hidden, grad_down = call(
        act_kernel,
        [sds((mb, slots, ff), F32)] * 3 + [sds((ff, width), BF)],
        6,
        2 * product,
        mb * slots * ff * 16,
        limit=32,
    )(me, gate_pre[:, 0], up_pre[:, 0], probs0, probs1, rows0, rows1)

    u = call(
        pair_kernel, [sds((n_x,) + piece, BF)], 1, 0, slots * ff * 2, has_me=False
    )(both)[0]
    u0 = lax.all_to_all(u, "x", 0, 0, tiled=True).reshape(slots, ff)
    u1 = lax.ppermute(u0, "core", SWAP)

    def slot(m, u_m, *before):
        return call(
            functools.partial(slot_kernel, nd, nq, mb, cap, m),
            [sds((slots, ff), BF), sds((slots, ff), BF), sds((nd * nq, line), BF)],
            6 + len(before),
            2 * product,
            slots * ff * 16,
            has_me=False,
        )(u_m, f_gate, f_up, hidden, w_gate, w_up, *before)

    dgate0, dup0, back = slot(0, u0)
    dgate1, dup1, back = slot(1, u1, back)
    home = lax.all_to_all(back.reshape(nd, nq, line), PLANE, 0, 0, tiled=True)
    part = call(
        functools.partial(unpack_kernel, dims),
        [sds((nq * toks, width + PAD), BF)],
        2,
        product // 4,
        nd * nq * line * 2,
    )(first, lines, home.reshape(nd * nq, line))[0]
    part = lax.all_to_all(part.reshape(n_a, mb * toks, width + PAD), "za", 0, 0, tiled=True)
    grad_gate, grad_up = call(
        weight_kernel, [sds((width, ff), BF)] * 2, 5, 4 * product, slots * ff * 12
    )(me, saved_inputs[:, 0], dgate0, dup0, dgate1, dup1)
    in_grad, prob_grad = call(
        total_kernel,
        [sds((mb, toks, width), BF), sds((mb, toks, top), BF)],
        1,
        0,
        toks * width * 20,
    )(me, part)
    return in_grad, prob_grad, grad_gate[None], grad_up[None], grad_down[None]


def solution(mesh):
    n_dp, n_ex = mesh.devices.shape
    n_a = 4 if n_ex >= 64 else 2
    fine = Mesh(
        mesh.devices.reshape(2, n_dp // 4, 2, n_a, n_ex // (4 * n_a), 4),
        ("zh", "x", "core", "za", "zb", "y"),
    )
    specs = (
        P(None, EX, DP),
        P(None, EX, None),
        P(None, EX, None),
        P(None, EX, None, DP),
        P(None, EX, None, None),
        P(None, EX, None, None),
        P(EX, DP, None),
        P(EX, DP, None),
        P(EX, None, DP),
    )
    return jax.shard_map(
        local,
        mesh=fine,
        in_specs=specs,
        out_specs=(specs[0], specs[1], specs[6], specs[7], specs[8]),
        check_vma=False,
    )
```

```python
import functools

import jax
import jax.numpy as jnp
from jax import lax
from jax.experimental import pallas as pl
from jax.experimental.pallas import tpu as pltpu
from jax.sharding import Mesh
from jax.sharding import PartitionSpec as P

BF = jnp.bfloat16
F32 = jnp.float32
DP = ("zh", "x", "core")
EX = ("za", "zb", "y")
PLANE = ("zb", "y")
PAD = 128
SWAP = [(0, 1), (1, 0)]
VMEM = pl.BlockSpec(memory_space=pltpu.VMEM)
SMEM = pl.BlockSpec(memory_space=pltpu.SMEM)


def dot(a, b, ca, cb):
    return lax.dot_general(a, b, (((ca,), (cb,)), ((), ())), preferred_element_type=F32)


def iota(shape, dim):
    return lax.broadcasted_iota(jnp.int32, shape, dim)


def call(body, outs, n_in, flops, bytes_moved, limit=24, has_me=True):
    first = [SMEM] if has_me else []
    return pl.pallas_call(
        body,
        out_shape=outs,
        in_specs=first + [VMEM] * n_in,
        out_specs=[VMEM] * len(outs),
        cost_estimate=pl.CostEstimate(flops=flops, bytes_accessed=bytes_moved, transcendentals=0),
        compiler_params=pltpu.CompilerParams(vmem_limit_bytes=limit << 20),
    )


def flat_kernel(me, ids, probs, rows, out):
    mb, toks, width = rows.shape
    top = ids.shape[1]
    ahead = iota((top, PAD), 1) - iota((top, PAD), 0)
    for m in range(mb):
        at = me[0] ^ m
        tail = dot(ids[at].astype(F32).astype(BF), (ahead == 0).astype(F32).astype(BF), 0, 0)
        tail = tail + dot(probs[at], (ahead == top).astype(F32).astype(BF), 0, 0)
        for peer in range(out.shape[0]):
            out[peer, m * toks : (m + 1) * toks, :width] = rows[at]
            out[peer, m * toks : (m + 1) * toks, width:] = tail.astype(BF)


def route_maps(names, first, size, nq, toks, cap):
    tokens, top = names.shape
    shape = (tokens, size)
    column = iota(shape, 1)
    expert = (first + lax.div(column, nq)).astype(F32)
    same = lax.div(iota(shape, 0), toks) == lax.rem(column, nq)
    picks = [jnp.where(same & (names[:, k : k + 1] == expert), 1.0, 0.0) for k in range(top)]
    hits = functools.reduce(jnp.add, picks)
    lower = jnp.where(iota((tokens, tokens), 0) > iota((tokens, tokens), 1), 1.0, 0.0)
    slot = dot(lower.astype(BF), hits.astype(BF), 1, 0)
    return picks, [jnp.where(slot == s, hits, 0.0) for s in range(cap)]


def pack_kernel(dims, first, lines, out):
    nd, nq, toks, top, cap, width = dims
    tail_in = lines[:, width:].astype(F32)
    picks, maps = route_maps(tail_in[:, :top], first[0], nd * nq, nq, toks, cap)
    grads = lines[:, :width]
    tokens = grads.shape[0]
    held = functools.reduce(
        jnp.add, [k * tail_in[:, top + i : top + i + 1] for i, k in enumerate(picks)]
    )
    tail = jnp.zeros((nd * nq, PAD), F32)
    for s, k in enumerate(maps):
        out[:, s * width : (s + 1) * width] = dot(k.astype(BF), grads, 0, 0).astype(BF)
        lane = jnp.where(iota((tokens, PAD), 1) == s, 1.0, 0.0).astype(BF)
        tail = tail + dot((k * held).astype(BF), lane, 0, 0)
    out[:, cap * width :] = tail.astype(BF)


def unpack_kernel(dims, first, lines, home, out):
    nd, nq, toks, top, cap, width = dims
    names = lines[:, width:].astype(F32)[:, :top]
    picks, maps = route_maps(names, first[0], nd * nq, nq, toks, cap)
    tokens = names.shape[0]
    total = jnp.zeros((tokens, width), F32)
    held = jnp.zeros((tokens, nd * nq), F32)
    tail = home[:, cap * width :]
    for s, k in enumerate(maps):
        total = total + dot(k.astype(BF), home[:, s * width : (s + 1) * width], 1, 0)
        lane = jnp.where(iota((tokens, PAD), 1) == s, 1.0, 0.0).astype(BF)
        held = held + k * dot(lane, tail, 1, 1)
    out[:, :width] = total.astype(BF)
    lane = iota((tokens, PAD), 1)
    picked = jnp.zeros((tokens, PAD), F32)
    for i, k in enumerate(picks):
        picked = jnp.where(lane == i, jnp.sum(k * held, axis=1, keepdims=True), picked)
    out[:, width:] = picked.astype(BF)


def total_kernel(me, parts, in_grad, prob_grad):
    mb, toks, width = in_grad.shape
    top = prob_grad.shape[1]
    column = (iota((top, PAD), 1) == iota((top, PAD), 0)).astype(F32).astype(BF)
    for m in range(mb):
        total = functools.reduce(
            jnp.add,
            [
                parts[i, m * toks : (m + 1) * toks, :].astype(F32)
                for i in range(parts.shape[0])
            ],
        )
        in_grad[me[0] ^ m] = total[:, :width].astype(BF)
        prob_grad[me[0] ^ m] = dot(column, total[:, width:].astype(BF), 1, 1).astype(BF)


def first_row(shape, nd, nq, mb, cap):
    column = iota(shape, 1)
    return (lax.div(lax.rem(column, nq), mb) * nd + lax.div(column, nq)) * cap


def spread(nd, nq, mb, cap, m, s=None):
    rows = (nd * nq // mb) * cap
    shape = (rows, nd * nq)
    ahead = iota(shape, 0) - first_row(shape, nd, nq, mb, cap)
    here = (ahead >= 0) & (ahead < cap) if s is None else ahead == s
    here = here & (lax.rem(iota(shape, 1), mb) == m)
    return jnp.where(here, 1.0, 0.0).astype(BF)


def down_kernel(nd, nq, mb, cap, m, got, w_down, part, rows, probs):
    slots, width = rows.shape
    total = jnp.zeros((slots, width), F32)
    for s in range(cap):
        total = total + dot(
            spread(nd, nq, mb, cap, m, s), got[:, s * width : (s + 1) * width], 1, 0
        )
    mine = total.astype(BF)
    rows[...] = mine
    part[...] = dot(mine, w_down[...], 1, 1)
    tail = dot(spread(nd, nq, mb, cap, m), got[:, cap * width :], 1, 0)
    shape = (slots, PAD)
    probs[...] = jnp.sum(
        jnp.where(iota(shape, 1) == lax.rem(iota(shape, 0), cap), tail, 0.0), axis=1, keepdims=True
    )


def sum_kernel(mine, own, others, out):
    n = others.shape[0]
    total = functools.reduce(
        jnp.add, [jnp.where(mine[0] == i, own[i], others[i].astype(F32)) for i in range(n)]
    )
    out[...] = total.astype(BF)


def pair_kernel(first, second, out):
    total = (first[...].astype(F32) + second[...].astype(F32)).astype(BF)
    for i in range(out.shape[0]):
        out[i] = total


def act_kernel(me, gate, up, probs0, probs1, rows0, rows1, f_gate, f_up, hidden, grad):
    total = None
    for m, (probs, rows) in enumerate(((probs0, rows0), (probs1, rows1))):
        gate_f = gate[me[0] ^ m].astype(F32)
        up_f = up[me[0] ^ m].astype(F32)
        p = probs[...]
        sig = 1.0 / (1.0 + jnp.exp(-gate_f))
        act = gate_f * sig
        h = act * up_f
        f_gate[m] = p * up_f * (sig * (1.0 + gate_f * (1.0 - sig)))
        f_up[m] = p * act
        hidden[m] = h
        term = dot((p * h).astype(BF), rows[...], 0, 0)
        total = term if total is None else total + term
    grad[...] = total.astype(BF)


def slot_kernel(nd, nq, mb, cap, m, u_ref, f_gate, f_up, hidden, w_gate, w_up, *rest):
    before, (dgate, dup, out) = rest[:-3], rest[-3:]
    u = u_ref[...].astype(F32)
    dg = (u * f_gate[m]).astype(BF)
    du = (u * f_up[m]).astype(BF)
    dgate[...] = dg
    dup[...] = du
    rows = (dot(dg, w_gate[...], 1, 1) + dot(du, w_up[...], 1, 1)).astype(BF)
    slots, width = rows.shape

    def put(low, high, value):
        if before:
            value = value + before[0][:, low:high].astype(F32)
        out[:, low:high] = value.astype(BF)

    for s in range(cap):
        put(s * width, (s + 1) * width, dot(spread(nd, nq, mb, cap, m, s), rows, 0, 0))
    slot_prob = jnp.sum(u * hidden[m], axis=1, keepdims=True)
    shape = (slots, PAD)
    tail = jnp.where(iota(shape, 1) == lax.rem(iota(shape, 0), cap), slot_prob, 0.0).astype(BF)
    put(cap * width, cap * width + PAD, dot(spread(nd, nq, mb, cap, m), tail, 0, 0))


def weight_kernel(me, inputs, dgate0, dup0, dgate1, dup1, grad_gate, grad_up):
    first, second = inputs[me[0]], inputs[me[0] ^ 1]
    grad_gate[...] = (dot(first, dgate0[...], 0, 0) + dot(second, dgate1[...], 0, 0)).astype(BF)
    grad_up[...] = (dot(first, dup0[...], 0, 0) + dot(second, dup1[...], 0, 0)).astype(BF)


def local(out_grad, expert_ids, probs, saved_inputs, gate_pre, up_pre, w_gate, w_up, w_down):
    sds = jax.ShapeDtypeStruct
    ne = lax.axis_size(EX)
    n_x = lax.axis_size("x")
    mb, toks, top = expert_ids.shape
    slots = saved_inputs.shape[2]
    cap = slots // ne
    width = out_grad.shape[2]
    ff = w_gate.shape[2]
    line = cap * width + PAD
    w_gate, w_up, w_down = w_gate[0], w_up[0], w_down[0]
    core = lax.axis_index("core")
    me = core.astype(jnp.int32).reshape(1)
    product = 2 * slots * width * ff

    n_a, nd = lax.axis_size("za"), lax.axis_size(PLANE)
    nq = n_a * mb
    dims = (nd, nq, toks, top, cap, width)
    first = (lax.axis_index("za").astype(jnp.int32) * nd).reshape(1)

    flat = call(flat_kernel, [sds((n_a, mb * toks, width + PAD), BF)], 3, 0, toks * width * 20)(
        me, jnp.swapaxes(expert_ids, 1, 2), jnp.swapaxes(probs, 1, 2), out_grad
    )[0]
    lines = lax.all_to_all(flat, "za", 0, 0, tiled=True).reshape(nq * toks, width + PAD)
    send = call(
        functools.partial(pack_kernel, dims), [sds((nd * nq, line), BF)], 1, product // 4, nd * nq * line * 2
    )(first, lines)[0]
    got = lax.all_to_all(send.reshape(nd, nq, line), PLANE, 0, 0, tiled=True).reshape(nd * nq, line)

    def down(m):
        return call(
            functools.partial(down_kernel, nd, nq, mb, cap, m),
            [sds((slots, ff), F32), sds((slots, width), BF), sds((slots, 1), F32)],
            2,
            product,
            slots * ff * 4,
            has_me=False,
        )(got, w_down)

    part1, rows1, probs1 = down(1)
    away = lax.ppermute(part1, "core", SWAP)
    part0, rows0, probs0 = down(0)
    half = (part0 + away).reshape(n_x, slots // n_x, ff)
    others = lax.all_to_all(half.astype(BF), "x", 0, 0, tiled=True)
    mine = lax.axis_index("x").astype(jnp.int32).reshape(1)
    piece = (slots // n_x, ff)
    eighth = call(
        sum_kernel, [sds(piece, BF)], 2, 0, slots * ff * 6
    )(mine, half, others)[0]
    other = lax.ppermute(eighth, "zh", SWAP)

    f_gate, f_up, hidden, grad_down = call(
        act_kernel,
        [sds((mb, slots, ff), F32)] * 3 + [sds((ff, width), BF)],
        6,
        2 * product,
        mb * slots * ff * 16,
        limit=32,
    )(me, gate_pre[:, 0], up_pre[:, 0], probs0, probs1, rows0, rows1)

    other, f_gate, f_up, hidden = lax.optimization_barrier((other, f_gate, f_up, hidden))
    u = call(
        pair_kernel, [sds((n_x,) + piece, BF)], 2, 0, slots * ff * 2, has_me=False
    )(eighth, other)[0]
    u0 = lax.all_to_all(u, "x", 0, 0, tiled=True).reshape(slots, ff)
    u1 = lax.ppermute(u0, "core", SWAP)

    def slot(m, u_m, *before):
        return call(
            functools.partial(slot_kernel, nd, nq, mb, cap, m),
            [sds((slots, ff), BF), sds((slots, ff), BF), sds((nd * nq, line), BF)],
            6 + len(before),
            2 * product,
            slots * ff * 16,
            has_me=False,
        )(u_m, f_gate, f_up, hidden, w_gate, w_up, *before)

    dgate0, dup0, back = slot(0, u0)
    dgate1, dup1, back = slot(1, u1, back)
    home = lax.all_to_all(back.reshape(nd, nq, line), PLANE, 0, 0, tiled=True)
    part = call(
        functools.partial(unpack_kernel, dims),
        [sds((nq * toks, width + PAD), BF)],
        2,
        product // 4,
        nd * nq * line * 2,
    )(first, lines, home.reshape(nd * nq, line))[0]
    part = lax.all_to_all(part.reshape(n_a, mb * toks, width + PAD), "za", 0, 0, tiled=True)
    grad_gate, grad_up = call(
        weight_kernel, [sds((width, ff), BF)] * 2, 5, 4 * product, slots * ff * 12
    )(me, saved_inputs[:, 0], dgate0, dup0, dgate1, dup1)
    in_grad, prob_grad = call(
        total_kernel,
        [sds((mb, toks, width), BF), sds((mb, top, toks), BF)],
        1,
        0,
        toks * width * 20,
    )(me, part)
    prob_grad = jnp.swapaxes(prob_grad, 1, 2)
    return in_grad, prob_grad, grad_gate[None], grad_up[None], grad_down[None]


def solution(mesh):
    n_dp, n_ex = mesh.devices.shape
    n_a = 4 if n_ex >= 64 else 2
    fine = Mesh(
        mesh.devices.reshape(2, n_dp // 4, 2, n_a, n_ex // (4 * n_a), 4),
        ("zh", "x", "core", "za", "zb", "y"),
    )
    specs = (
        P(None, EX, DP),
        P(None, EX, None),
        P(None, EX, None),
        P(None, EX, None, DP),
        P(None, EX, None, None),
        P(None, EX, None, None),
        P(EX, DP, None),
        P(EX, DP, None),
        P(EX, None, DP),
    )
    return jax.shard_map(
        local,
        mesh=fine,
        in_specs=specs,
        out_specs=(specs[0], specs[1], specs[6], specs[7], specs[8]),
        check_vma=False,
    )
```

```python
import functools

import jax
import jax.numpy as jnp
from jax import lax
from jax.experimental import pallas as pl
from jax.experimental.pallas import tpu as pltpu
from jax.sharding import Mesh
from jax.sharding import PartitionSpec as P

BF = jnp.bfloat16
F32 = jnp.float32
DP = ("zh", "x", "core")
EX = ("za", "zb", "y")
PLANE = ("zb", "y")
PAD = 128
SWAP = [(0, 1), (1, 0)]
VMEM = pl.BlockSpec(memory_space=pltpu.VMEM)
SMEM = pl.BlockSpec(memory_space=pltpu.SMEM)


def dot(a, b, ca, cb):
    return lax.dot_general(a, b, (((ca,), (cb,)), ((), ())), preferred_element_type=F32)


def iota(shape, dim):
    return lax.broadcasted_iota(jnp.int32, shape, dim)


def call(body, outs, n_in, flops, bytes_moved, limit=24, has_me=True):
    first = [SMEM] if has_me else []
    return pl.pallas_call(
        body,
        out_shape=outs,
        in_specs=first + [VMEM] * n_in,
        out_specs=[VMEM] * len(outs),
        cost_estimate=pl.CostEstimate(flops=flops, bytes_accessed=bytes_moved, transcendentals=0),
        compiler_params=pltpu.CompilerParams(vmem_limit_bytes=limit << 20),
    )


def flat_kernel(me, ids, probs, rows, out):
    mb, toks, width = rows.shape
    top = ids.shape[1]
    ahead = iota((top, PAD), 1) - iota((top, PAD), 0)
    tail = jnp.zeros((toks, PAD), F32)
    for m in range(mb):
        at = me[0] ^ m
        base = 2 * m * top
        for offset, value in ((base, ids[at].astype(F32).astype(BF)), (base + top, probs[at])):
            tail = tail + dot(value, (ahead == offset).astype(F32).astype(BF), 0, 0)
        for peer in range(out.shape[0]):
            out[peer, :, m * width : (m + 1) * width] = rows[at]
    for peer in range(out.shape[0]):
        out[peer, :, mb * width :] = tail.astype(BF)


def route_maps(names, first, size, nq, toks, cap):
    tokens, top = names.shape
    shape = (tokens, size)
    column = iota(shape, 1)
    expert = (first + lax.div(column, nq)).astype(F32)
    same = lax.div(iota(shape, 0), toks) == lax.rem(column, nq)
    picks = [jnp.where(same & (names[:, k : k + 1] == expert), 1.0, 0.0) for k in range(top)]
    hits = functools.reduce(jnp.add, picks)
    lower = jnp.where(iota((tokens, tokens), 0) > iota((tokens, tokens), 1), 1.0, 0.0)
    slot = dot(lower.astype(BF), hits.astype(BF), 1, 0)
    return picks, [jnp.where(slot == s, hits, 0.0) for s in range(cap)]


def small_lines(lines, mb, top, width):
    tail = lines[:, mb * width :]
    shape = (PAD, PAD)
    parts = []
    for m in range(mb):
        move = (iota(shape, 0) == iota(shape, 1) + 2 * m * top).astype(F32).astype(BF)
        parts.append(dot(tail, move, 1, 0))
    return jnp.concatenate(parts, axis=0)


def pack_kernel(dims, first, lines, out):
    nd, nq, mb, toks, top, cap, width = dims
    tail_in = small_lines(lines, mb, top, width)
    picks, maps = route_maps(tail_in[:, :top], first[0], nd * nq, nq, toks, cap)
    grads = jnp.concatenate([lines[:, m * width : (m + 1) * width] for m in range(mb)], axis=0)
    tokens = grads.shape[0]
    held = functools.reduce(
        jnp.add, [k * tail_in[:, top + i : top + i + 1] for i, k in enumerate(picks)]
    )
    tail = jnp.zeros((nd * nq, PAD), F32)
    for s, k in enumerate(maps):
        out[:, s * width : (s + 1) * width] = dot(k.astype(BF), grads, 0, 0).astype(BF)
        lane = jnp.where(iota((tokens, PAD), 1) == s, 1.0, 0.0).astype(BF)
        tail = tail + dot((k * held).astype(BF), lane, 0, 0)
    out[:, cap * width :] = tail.astype(BF)


def unpack_kernel(dims, first, lines, home, out):
    nd, nq, mb, toks, top, cap, width = dims
    names = small_lines(lines, mb, top, width)[:, :top]
    picks, maps = route_maps(names, first[0], nd * nq, nq, toks, cap)
    tokens = names.shape[0]
    total = jnp.zeros((tokens, width), F32)
    held = jnp.zeros((tokens, nd * nq), F32)
    tail = home[:, cap * width :]
    for s, k in enumerate(maps):
        total = total + dot(k.astype(BF), home[:, s * width : (s + 1) * width], 1, 0)
        lane = jnp.where(iota((tokens, PAD), 1) == s, 1.0, 0.0).astype(BF)
        held = held + k * dot(lane, tail, 1, 1)
    run = tokens // mb
    lane = iota((run, PAD), 1)
    picked = jnp.zeros((run, PAD), F32)
    for m in range(mb):
        at = slice(m * run, (m + 1) * run)
        out[:, m * width : (m + 1) * width] = total[at].astype(BF)
        for i, k in enumerate(picks):
            value = jnp.sum(k[at] * held[at], axis=1, keepdims=True)
            picked = jnp.where(lane == m * top + i, value, picked)
    out[:, mb * width :] = picked.astype(BF)


def total_kernel(me, parts, in_grad, prob_grad):
    mb, toks, width = in_grad.shape
    top = prob_grad.shape[1]
    total = functools.reduce(jnp.add, [parts[i].astype(F32) for i in range(parts.shape[0])])
    tail = total[:, mb * width :].astype(BF)
    ahead = iota((top, PAD), 1) - iota((top, PAD), 0)
    for m in range(mb):
        in_grad[me[0] ^ m] = total[:, m * width : (m + 1) * width].astype(BF)
        column = (ahead == m * top).astype(F32).astype(BF)
        prob_grad[me[0] ^ m] = dot(column, tail, 1, 1).astype(BF)


def first_row(shape, nd, nq, mb, cap):
    column = iota(shape, 1)
    return (lax.rem(lax.rem(column, nq), nq // mb) * nd + lax.div(column, nq)) * cap


def spread(nd, nq, mb, cap, m, s=None):
    rows = (nd * nq // mb) * cap
    shape = (rows, nd * nq)
    ahead = iota(shape, 0) - first_row(shape, nd, nq, mb, cap)
    here = (ahead >= 0) & (ahead < cap) if s is None else ahead == s
    here = here & (lax.div(lax.rem(iota(shape, 1), nq), nq // mb) == m)
    return jnp.where(here, 1.0, 0.0).astype(BF)


def down_kernel(nd, nq, mb, cap, m, got, w_down, part, rows, probs):
    slots, width = rows.shape
    total = jnp.zeros((slots, width), F32)
    for s in range(cap):
        total = total + dot(
            spread(nd, nq, mb, cap, m, s), got[:, s * width : (s + 1) * width], 1, 0
        )
    mine = total.astype(BF)
    rows[...] = mine
    part[...] = dot(mine, w_down[...], 1, 1)
    tail = dot(spread(nd, nq, mb, cap, m), got[:, cap * width :], 1, 0)
    shape = (slots, PAD)
    probs[...] = jnp.sum(
        jnp.where(iota(shape, 1) == lax.rem(iota(shape, 0), cap), tail, 0.0), axis=1, keepdims=True
    )


def sum_kernel(mine, own, others, out):
    n = others.shape[0]
    total = functools.reduce(
        jnp.add, [jnp.where(mine[0] == i, own[i], others[i].astype(F32)) for i in range(n)]
    )
    out[...] = total.astype(BF)


def pair_kernel(first, second, out):
    total = (first[...].astype(F32) + second[...].astype(F32)).astype(BF)
    for i in range(out.shape[0]):
        out[i] = total


def act_kernel(me, gate, up, probs0, probs1, rows0, rows1, f_gate, f_up, hidden, grad):
    total = None
    for m, (probs, rows) in enumerate(((probs0, rows0), (probs1, rows1))):
        gate_f = gate[me[0] ^ m].astype(F32)
        up_f = up[me[0] ^ m].astype(F32)
        p = probs[...]
        sig = 1.0 / (1.0 + jnp.exp(-gate_f))
        act = gate_f * sig
        h = act * up_f
        f_gate[m] = p * up_f * (sig * (1.0 + gate_f * (1.0 - sig)))
        f_up[m] = p * act
        hidden[m] = h
        term = dot((p * h).astype(BF), rows[...], 0, 0)
        total = term if total is None else total + term
    grad[...] = total.astype(BF)


def slot_kernel(nd, nq, mb, cap, m, u_ref, f_gate, f_up, hidden, w_gate, w_up, *rest):
    before, (dgate, dup, out) = rest[:-3], rest[-3:]
    u = u_ref[...].astype(F32)
    dg = (u * f_gate[m]).astype(BF)
    du = (u * f_up[m]).astype(BF)
    dgate[...] = dg
    dup[...] = du
    rows = (dot(dg, w_gate[...], 1, 1) + dot(du, w_up[...], 1, 1)).astype(BF)
    slots, width = rows.shape

    def put(low, high, value):
        if before:
            value = value + before[0][:, low:high].astype(F32)
        out[:, low:high] = value.astype(BF)

    for s in range(cap):
        put(s * width, (s + 1) * width, dot(spread(nd, nq, mb, cap, m, s), rows, 0, 0))
    slot_prob = jnp.sum(u * hidden[m], axis=1, keepdims=True)
    shape = (slots, PAD)
    tail = jnp.where(iota(shape, 1) == lax.rem(iota(shape, 0), cap), slot_prob, 0.0).astype(BF)
    put(cap * width, cap * width + PAD, dot(spread(nd, nq, mb, cap, m), tail, 0, 0))


def weight_kernel(me, inputs, dgate0, dup0, dgate1, dup1, grad_gate, grad_up):
    first, second = inputs[me[0]], inputs[me[0] ^ 1]
    grad_gate[...] = (dot(first, dgate0[...], 0, 0) + dot(second, dgate1[...], 0, 0)).astype(BF)
    grad_up[...] = (dot(first, dup0[...], 0, 0) + dot(second, dup1[...], 0, 0)).astype(BF)


def local(out_grad, expert_ids, probs, saved_inputs, gate_pre, up_pre, w_gate, w_up, w_down):
    sds = jax.ShapeDtypeStruct
    ne = lax.axis_size(EX)
    n_x = lax.axis_size("x")
    mb, toks, top = expert_ids.shape
    slots = saved_inputs.shape[2]
    cap = slots // ne
    width = out_grad.shape[2]
    ff = w_gate.shape[2]
    line = cap * width + PAD
    w_gate, w_up, w_down = w_gate[0], w_up[0], w_down[0]
    core = lax.axis_index("core")
    me = core.astype(jnp.int32).reshape(1)
    product = 2 * slots * width * ff

    n_a, nd = lax.axis_size("za"), lax.axis_size(PLANE)
    nq = n_a * mb
    dims = (nd, nq, mb, toks, top, cap, width)
    wide = mb * width + PAD
    first = (lax.axis_index("za").astype(jnp.int32) * nd).reshape(1)

    flat = call(flat_kernel, [sds((n_a, toks, wide), BF)], 3, 0, toks * width * 20)(
        me, jnp.swapaxes(expert_ids, 1, 2), jnp.swapaxes(probs, 1, 2), out_grad
    )[0]
    lines = lax.all_to_all(flat, "za", 0, 0, tiled=True).reshape(n_a * toks, wide)
    send = call(
        functools.partial(pack_kernel, dims), [sds((nd * nq, line), BF)], 1, product // 4, nd * nq * line * 2
    )(first, lines)[0]
    got = lax.all_to_all(send.reshape(nd, nq, line), PLANE, 0, 0, tiled=True).reshape(nd * nq, line)

    def down(m):
        return call(
            functools.partial(down_kernel, nd, nq, mb, cap, m),
            [sds((slots, ff), F32), sds((slots, width), BF), sds((slots, 1), F32)],
            2,
            product,
            slots * ff * 4,
            has_me=False,
        )(got, w_down)

    part1, rows1, probs1 = down(1)
    away = lax.ppermute(part1, "core", SWAP)
    part0, rows0, probs0 = down(0)
    half = (part0 + away).reshape(n_x, slots // n_x, ff)
    others = lax.all_to_all(half.astype(BF), "x", 0, 0, tiled=True)
    mine = lax.axis_index("x").astype(jnp.int32).reshape(1)
    piece = (slots // n_x, ff)
    eighth = call(
        sum_kernel, [sds(piece, BF)], 2, 0, slots * ff * 6
    )(mine, half, others)[0]
    other = lax.ppermute(eighth, "zh", SWAP)

    f_gate, f_up, hidden, grad_down = call(
        act_kernel,
        [sds((mb, slots, ff), F32)] * 3 + [sds((ff, width), BF)],
        6,
        2 * product,
        mb * slots * ff * 16,
        limit=32,
    )(me, gate_pre[:, 0], up_pre[:, 0], probs0, probs1, rows0, rows1)

    other, f_gate, f_up, hidden = lax.optimization_barrier((other, f_gate, f_up, hidden))
    u = call(
        pair_kernel, [sds((n_x,) + piece, BF)], 2, 0, slots * ff * 2, has_me=False
    )(eighth, other)[0]
    u0 = lax.all_to_all(u, "x", 0, 0, tiled=True).reshape(slots, ff)
    u1 = lax.ppermute(u0, "core", SWAP)

    def slot(m, u_m, *before):
        return call(
            functools.partial(slot_kernel, nd, nq, mb, cap, m),
            [sds((slots, ff), BF), sds((slots, ff), BF), sds((nd * nq, line), BF)],
            6 + len(before),
            2 * product,
            slots * ff * 16,
            has_me=False,
        )(u_m, f_gate, f_up, hidden, w_gate, w_up, *before)

    dgate0, dup0, back = slot(0, u0)
    dgate1, dup1, back = slot(1, u1, back)
    home = lax.all_to_all(back.reshape(nd, nq, line), PLANE, 0, 0, tiled=True)
    part = call(
        functools.partial(unpack_kernel, dims),
        [sds((n_a * toks, wide), BF)],
        2,
        product // 4,
        nd * nq * line * 2,
    )(first, lines, home.reshape(nd * nq, line))[0]
    part = lax.all_to_all(part.reshape(n_a, toks, wide), "za", 0, 0, tiled=True)
    grad_gate, grad_up = call(
        weight_kernel, [sds((width, ff), BF)] * 2, 5, 4 * product, slots * ff * 12
    )(me, saved_inputs[:, 0], dgate0, dup0, dgate1, dup1)
    in_grad, prob_grad = call(
        total_kernel,
        [sds((mb, toks, width), BF), sds((mb, top, toks), BF)],
        1,
        0,
        toks * width * 20,
    )(me, part)
    prob_grad = jnp.swapaxes(prob_grad, 1, 2)
    return in_grad, prob_grad, grad_gate[None], grad_up[None], grad_down[None]


def solution(mesh):
    n_dp, n_ex = mesh.devices.shape
    n_a = 4 if n_ex >= 64 else 2
    fine = Mesh(
        mesh.devices.reshape(2, n_dp // 4, 2, n_a, n_ex // (4 * n_a), 4),
        ("zh", "x", "core", "za", "zb", "y"),
    )
    specs = (
        P(None, EX, DP),
        P(None, EX, None),
        P(None, EX, None),
        P(None, EX, None, DP),
        P(None, EX, None, None),
        P(None, EX, None, None),
        P(EX, DP, None),
        P(EX, DP, None),
        P(EX, None, DP),
    )
    return jax.shard_map(
        local,
        mesh=fine,
        in_specs=specs,
        out_specs=(specs[0], specs[1], specs[6], specs[7], specs[8]),
        check_vma=False,
    )
```

```python
import functools

import jax
import jax.numpy as jnp
from jax import lax
from jax.experimental import pallas as pl
from jax.experimental.pallas import tpu as pltpu
from jax.sharding import Mesh
from jax.sharding import PartitionSpec as P

BF = jnp.bfloat16
F32 = jnp.float32
DP = ("zh", "x", "core")
EX = ("za", "zb", "y")
PLANE = ("zb", "y")
PAD = 128
SWAP = [(0, 1), (1, 0)]
VMEM = pl.BlockSpec(memory_space=pltpu.VMEM)
SMEM = pl.BlockSpec(memory_space=pltpu.SMEM)


def dot(a, b, ca, cb):
    return lax.dot_general(a, b, (((ca,), (cb,)), ((), ())), preferred_element_type=F32)


def iota(shape, dim):
    return lax.broadcasted_iota(jnp.int32, shape, dim)


def call(body, outs, n_in, flops, bytes_moved, limit=24, has_me=True):
    first = [SMEM] if has_me else []
    return pl.pallas_call(
        body,
        out_shape=outs,
        in_specs=first + [VMEM] * n_in,
        out_specs=[VMEM] * len(outs),
        cost_estimate=pl.CostEstimate(flops=flops, bytes_accessed=bytes_moved, transcendentals=0),
        compiler_params=pltpu.CompilerParams(vmem_limit_bytes=limit << 20),
    )


def flat_kernel(me, ids_in, probs_in, rows_in, out, ids, probs, rows, sems):
    copies = [
        pltpu.make_async_copy(source, held, sems.at[i])
        for i, (source, held) in enumerate(((ids_in, ids), (probs_in, probs), (rows_in, rows)))
    ]
    for copy in copies:
        copy.start()
    for copy in copies:
        copy.wait()
    mb, toks, width = rows.shape
    top = ids.shape[1]
    ahead = iota((top, PAD), 1) - iota((top, PAD), 0)
    tail = jnp.zeros((toks, PAD), F32)
    for m in range(mb):
        at = me[0] ^ m
        base = 2 * m * top
        for offset, value in ((base, ids[at].astype(F32).astype(BF)), (base + top, probs[at])):
            tail = tail + dot(value, (ahead == offset).astype(F32).astype(BF), 0, 0)
        for peer in range(out.shape[0]):
            out[peer, :, m * width : (m + 1) * width] = rows[at]
    for peer in range(out.shape[0]):
        out[peer, :, mb * width :] = tail.astype(BF)


def route_maps(names, first, size, nq, toks, cap):
    tokens, top = names.shape
    shape = (tokens, size)
    column = iota(shape, 1)
    expert = (first + lax.div(column, nq)).astype(F32)
    same = lax.div(iota(shape, 0), toks) == lax.rem(column, nq)
    picks = [jnp.where(same & (names[:, k : k + 1] == expert), 1.0, 0.0) for k in range(top)]
    hits = functools.reduce(jnp.add, picks)
    lower = jnp.where(iota((tokens, tokens), 0) > iota((tokens, tokens), 1), 1.0, 0.0)
    slot = dot(lower.astype(BF), hits.astype(BF), 1, 0)
    return picks, [jnp.where(slot == s, hits, 0.0) for s in range(cap)]


def small_lines(lines, mb, top, width):
    tail = lines[:, mb * width :]
    shape = (PAD, PAD)
    parts = []
    for m in range(mb):
        move = (iota(shape, 0) == iota(shape, 1) + 2 * m * top).astype(F32).astype(BF)
        parts.append(dot(tail, move, 1, 0))
    return jnp.concatenate(parts, axis=0)


def pack_kernel(dims, first, lines, out):
    nd, nq, mb, toks, top, cap, width = dims
    tail_in = small_lines(lines, mb, top, width)
    picks, maps = route_maps(tail_in[:, :top], first[0], nd * nq, nq, toks, cap)
    grads = jnp.concatenate([lines[:, m * width : (m + 1) * width] for m in range(mb)], axis=0)
    tokens = grads.shape[0]
    held = functools.reduce(
        jnp.add, [k * tail_in[:, top + i : top + i + 1] for i, k in enumerate(picks)]
    )
    tail = jnp.zeros((nd * nq, PAD), F32)
    for s, k in enumerate(maps):
        out[:, s * width : (s + 1) * width] = dot(k.astype(BF), grads, 0, 0).astype(BF)
        lane = jnp.where(iota((tokens, PAD), 1) == s, 1.0, 0.0).astype(BF)
        tail = tail + dot((k * held).astype(BF), lane, 0, 0)
    out[:, cap * width :] = tail.astype(BF)


def unpack_kernel(dims, first, lines, home, out):
    nd, nq, mb, toks, top, cap, width = dims
    names = small_lines(lines, mb, top, width)[:, :top]
    picks, maps = route_maps(names, first[0], nd * nq, nq, toks, cap)
    tokens = names.shape[0]
    total = jnp.zeros((tokens, width), F32)
    held = jnp.zeros((tokens, nd * nq), F32)
    tail = home[:, cap * width :]
    for s, k in enumerate(maps):
        total = total + dot(k.astype(BF), home[:, s * width : (s + 1) * width], 1, 0)
        lane = jnp.where(iota((tokens, PAD), 1) == s, 1.0, 0.0).astype(BF)
        held = held + k * dot(lane, tail, 1, 1)
    run = tokens // mb
    shape = (nd * nq, PAD)
    picked = jnp.zeros((run, PAD), F32)
    for i, k in enumerate(picks):
        value = (k * held).astype(BF)
        for m in range(mb):
            lane = (iota(shape, 1) == m * top + i).astype(F32).astype(BF)
            picked = picked + dot(value[m * run : (m + 1) * run], lane, 1, 0)
    for m in range(mb):
        out[:, m * width : (m + 1) * width] = total[m * run : (m + 1) * run].astype(BF)
    out[:, mb * width :] = picked.astype(BF)


def total_kernel(me, parts, in_grad, prob_grad):
    mb, toks, width = in_grad.shape
    top = prob_grad.shape[1]
    total = functools.reduce(jnp.add, [parts[i].astype(F32) for i in range(parts.shape[0])])
    tail = total[:, mb * width :].astype(BF)
    ahead = iota((top, PAD), 1) - iota((top, PAD), 0)
    for m in range(mb):
        in_grad[me[0] ^ m] = total[:, m * width : (m + 1) * width].astype(BF)
        column = (ahead == m * top).astype(F32).astype(BF)
        prob_grad[me[0] ^ m] = dot(column, tail, 1, 1).astype(BF)


def first_row(shape, nd, nq, mb, cap):
    column = iota(shape, 1)
    return (lax.rem(lax.rem(column, nq), nq // mb) * nd + lax.div(column, nq)) * cap


def spread(nd, nq, mb, cap, m, s=None):
    rows = (nd * nq // mb) * cap
    shape = (rows, nd * nq)
    ahead = iota(shape, 0) - first_row(shape, nd, nq, mb, cap)
    here = (ahead >= 0) & (ahead < cap) if s is None else ahead == s
    here = here & (lax.div(lax.rem(iota(shape, 1), nq), nq // mb) == m)
    return jnp.where(here, 1.0, 0.0).astype(BF)


def down_kernel(nd, nq, mb, cap, m, got, w_down, part, rows, probs):
    slots, width = rows.shape
    total = jnp.zeros((slots, width), F32)
    for s in range(cap):
        total = total + dot(
            spread(nd, nq, mb, cap, m, s), got[:, s * width : (s + 1) * width], 1, 0
        )
    mine = total.astype(BF)
    rows[...] = mine
    part[...] = dot(mine, w_down[...], 1, 1)
    tail = dot(spread(nd, nq, mb, cap, m), got[:, cap * width :], 1, 0)
    shape = (slots, PAD)
    probs[...] = jnp.sum(
        jnp.where(iota(shape, 1) == lax.rem(iota(shape, 0), cap), tail, 0.0), axis=1, keepdims=True
    )


def join_kernel(part, away, out):
    out[...] = (part[...] + away[...]).astype(BF)


def sum_kernel(mine, part, away, others, out):
    rows = out.shape[0]
    at = pl.ds(pl.multiple_of(mine[0] * rows, 8), rows)
    total = part[at, :] + away[at, :]
    for i in range(others.shape[0]):
        total = total + jnp.where(mine[0] == i, 0.0, others[i].astype(F32))
    out[...] = total.astype(BF)


def pair_kernel(first, second, out):
    total = (first[...].astype(F32) + second[...].astype(F32)).astype(BF)
    for i in range(out.shape[0]):
        out[i] = total


def act_kernel(me, gate, up, probs0, probs1, rows0, rows1, f_gate, f_up, hidden, grad):
    total = None
    for m, (probs, rows) in enumerate(((probs0, rows0), (probs1, rows1))):
        gate_f = gate[me[0] ^ m].astype(F32)
        up_f = up[me[0] ^ m].astype(F32)
        p = probs[...]
        sig = 1.0 / (1.0 + jnp.exp(-gate_f))
        act = gate_f * sig
        h = act * up_f
        f_gate[m] = p * up_f * (sig * (1.0 + gate_f * (1.0 - sig)))
        f_up[m] = p * act
        hidden[m] = h
        term = dot((p * h).astype(BF), rows[...], 0, 0)
        total = term if total is None else total + term
    grad[...] = total.astype(BF)


def slot_kernel(nd, nq, mb, cap, m, u_ref, f_gate, f_up, hidden, w_gate, w_up, *rest):
    before, (dgate, dup, out) = rest[:-3], rest[-3:]
    u = u_ref[...].astype(F32)
    dg = (u * f_gate[m]).astype(BF)
    du = (u * f_up[m]).astype(BF)
    dgate[...] = dg
    dup[...] = du
    rows = (dot(dg, w_gate[...], 1, 1) + dot(du, w_up[...], 1, 1)).astype(BF)
    slots, width = rows.shape

    def put(low, high, value):
        if before:
            value = value + before[0][:, low:high].astype(F32)
        out[:, low:high] = value.astype(BF)

    for s in range(cap):
        put(s * width, (s + 1) * width, dot(spread(nd, nq, mb, cap, m, s), rows, 0, 0))
    slot_prob = jnp.sum(u * hidden[m], axis=1, keepdims=True)
    shape = (slots, PAD)
    tail = jnp.where(iota(shape, 1) == lax.rem(iota(shape, 0), cap), slot_prob, 0.0).astype(BF)
    put(cap * width, cap * width + PAD, dot(spread(nd, nq, mb, cap, m), tail, 0, 0))


def weight_kernel(me, inputs, dgate0, dup0, dgate1, dup1, grad_gate, grad_up):
    first, second = inputs[me[0]], inputs[me[0] ^ 1]
    grad_gate[...] = (dot(first, dgate0[...], 0, 0) + dot(second, dgate1[...], 0, 0)).astype(BF)
    grad_up[...] = (dot(first, dup0[...], 0, 0) + dot(second, dup1[...], 0, 0)).astype(BF)


def local(out_grad, expert_ids, probs, saved_inputs, gate_pre, up_pre, w_gate, w_up, w_down):
    sds = jax.ShapeDtypeStruct
    ne = lax.axis_size(EX)
    n_x = lax.axis_size("x")
    mb, toks, top = expert_ids.shape
    slots = saved_inputs.shape[2]
    cap = slots // ne
    width = out_grad.shape[2]
    ff = w_gate.shape[2]
    line = cap * width + PAD
    w_gate, w_up, w_down = w_gate[0], w_up[0], w_down[0]
    core = lax.axis_index("core")
    me = core.astype(jnp.int32).reshape(1)
    product = 2 * slots * width * ff

    n_a, nd = lax.axis_size("za"), lax.axis_size(PLANE)
    nq = n_a * mb
    dims = (nd, nq, mb, toks, top, cap, width)
    wide = mb * width + PAD
    first = (lax.axis_index("za").astype(jnp.int32) * nd).reshape(1)

    hbm = pl.BlockSpec(memory_space=pltpu.HBM)
    flat = pl.pallas_call(
        flat_kernel,
        out_shape=sds((n_a, toks, wide), BF),
        in_specs=[SMEM, hbm, hbm, hbm],
        out_specs=VMEM,
        scratch_shapes=[
            pltpu.VMEM((mb, top, toks), jnp.int32),
            pltpu.VMEM((mb, top, toks), BF),
            pltpu.VMEM((mb, toks, width), BF),
            pltpu.SemaphoreType.DMA((3,)),
        ],
        compiler_params=pltpu.CompilerParams(vmem_limit_bytes=56 << 20),
    )(me, jnp.swapaxes(expert_ids, 1, 2), jnp.swapaxes(probs, 1, 2), out_grad)
    lines = lax.all_to_all(flat, "za", 0, 0, tiled=True).reshape(n_a * toks, wide)
    send = call(
        functools.partial(pack_kernel, dims), [sds((nd * nq, line), BF)], 1, product // 4, nd * nq * line * 2
    )(first, lines)[0]
    got = lax.all_to_all(send.reshape(nd, nq, line), PLANE, 0, 0, tiled=True).reshape(nd * nq, line)

    def down(m):
        return call(
            functools.partial(down_kernel, nd, nq, mb, cap, m),
            [sds((slots, ff), F32), sds((slots, width), BF), sds((slots, 1), F32)],
            2,
            product,
            slots * ff * 4,
            has_me=False,
        )(got, w_down)

    part1, rows1, probs1 = down(1)
    away = lax.ppermute(part1, "core", SWAP)
    part0, rows0, probs0 = down(0)
    half = call(join_kernel, [sds((slots, ff), BF)], 2, 0, slots * ff * 10, has_me=False)(
        part0, away
    )[0]
    others = lax.all_to_all(half.reshape(n_x, slots // n_x, ff), "x", 0, 0, tiled=True)
    mine = lax.axis_index("x").astype(jnp.int32).reshape(1)
    piece = (slots // n_x, ff)
    eighth = call(
        sum_kernel, [sds(piece, BF)], 3, 0, slots * ff * 4
    )(mine, part0, away, others)[0]
    other = lax.ppermute(eighth, "zh", SWAP)

    f_gate, f_up, hidden, grad_down = call(
        act_kernel,
        [sds((mb, slots, ff), F32)] * 3 + [sds((ff, width), BF)],
        6,
        2 * product,
        mb * slots * ff * 16,
        limit=32,
    )(me, gate_pre[:, 0], up_pre[:, 0], probs0, probs1, rows0, rows1)

    other, f_gate, f_up, hidden = lax.optimization_barrier((other, f_gate, f_up, hidden))
    u = call(
        pair_kernel, [sds((n_x,) + piece, BF)], 2, 0, slots * ff * 2, has_me=False
    )(eighth, other)[0]
    u0 = lax.all_to_all(u, "x", 0, 0, tiled=True).reshape(slots, ff)
    u1 = lax.ppermute(u0, "core", SWAP)

    def slot(m, u_m, *before):
        return call(
            functools.partial(slot_kernel, nd, nq, mb, cap, m),
            [sds((slots, ff), BF), sds((slots, ff), BF), sds((nd * nq, line), BF)],
            6 + len(before),
            2 * product,
            slots * ff * 16,
            has_me=False,
        )(u_m, f_gate, f_up, hidden, w_gate, w_up, *before)

    dgate0, dup0, back = slot(0, u0)
    dgate1, dup1, back = slot(1, u1, back)
    home = lax.all_to_all(back.reshape(nd, nq, line), PLANE, 0, 0, tiled=True)
    part = call(
        functools.partial(unpack_kernel, dims),
        [sds((n_a * toks, wide), BF)],
        2,
        product // 4,
        nd * nq * line * 2,
    )(first, lines, home.reshape(nd * nq, line))[0]
    part = lax.all_to_all(part.reshape(n_a, toks, wide), "za", 0, 0, tiled=True)
    grad_gate, grad_up = call(
        weight_kernel, [sds((width, ff), BF)] * 2, 5, 4 * product, slots * ff * 12
    )(me, saved_inputs[:, 0], dgate0, dup0, dgate1, dup1)
    in_grad, prob_grad = call(
        total_kernel,
        [sds((mb, toks, width), BF), sds((mb, top, toks), BF)],
        1,
        0,
        toks * width * 20,
    )(me, part)
    prob_grad = jnp.swapaxes(prob_grad, 1, 2)
    return in_grad, prob_grad, grad_gate[None], grad_up[None], grad_down[None]


def solution(mesh):
    n_dp, n_ex = mesh.devices.shape
    n_a = 4 if n_ex >= 64 else 2
    fine = Mesh(
        mesh.devices.reshape(2, n_dp // 4, 2, n_a, n_ex // (4 * n_a), 4),
        ("zh", "x", "core", "za", "zb", "y"),
    )
    specs = (
        P(None, EX, DP),
        P(None, EX, None),
        P(None, EX, None),
        P(None, EX, None, DP),
        P(None, EX, None, None),
        P(None, EX, None, None),
        P(EX, DP, None),
        P(EX, DP, None),
        P(EX, None, DP),
    )
    return jax.shard_map(
        local,
        mesh=fine,
        in_specs=specs,
        out_specs=(specs[0], specs[1], specs[6], specs[7], specs[8]),
        check_vma=False,
    )
```

```python
import functools

import jax
import jax.numpy as jnp
from jax import lax
from jax.experimental import pallas as pl
from jax.experimental.pallas import tpu as pltpu
from jax.sharding import Mesh
from jax.sharding import PartitionSpec as P

BF = jnp.bfloat16
F32 = jnp.float32
DP = ("zh", "x", "core")
EX = ("za", "zb", "y")
PLANE = ("zb", "y")
PAD = 128
SWAP = [(0, 1), (1, 0)]
VMEM = pl.BlockSpec(memory_space=pltpu.VMEM)
SMEM = pl.BlockSpec(memory_space=pltpu.SMEM)


def dot(a, b, ca, cb):
    return lax.dot_general(a, b, (((ca,), (cb,)), ((), ())), preferred_element_type=F32)


def iota(shape, dim):
    return lax.broadcasted_iota(jnp.int32, shape, dim)


def call(body, outs, n_in, flops, bytes_moved, limit=24, has_me=True):
    first = [SMEM] if has_me else []
    return pl.pallas_call(
        body,
        out_shape=outs,
        in_specs=first + [VMEM] * n_in,
        out_specs=[VMEM] * len(outs),
        cost_estimate=pl.CostEstimate(flops=flops, bytes_accessed=bytes_moved, transcendentals=0),
        compiler_params=pltpu.CompilerParams(vmem_limit_bytes=limit << 20),
    )


def flat_kernel(me, ids_in, probs_in, rows_in, out, ids, probs, rows, sems):
    copies = [
        pltpu.make_async_copy(source, held, sems.at[i])
        for i, (source, held) in enumerate(((ids_in, ids), (probs_in, probs), (rows_in, rows)))
    ]
    for copy in copies:
        copy.start()
    for copy in copies:
        copy.wait()
    mb, toks, width = rows.shape
    top = ids.shape[1]
    ahead = iota((top, PAD), 1) - iota((top, PAD), 0)
    tail = jnp.zeros((toks, PAD), F32)
    for m in range(mb):
        at = me[0] ^ m
        base = 2 * m * top
        for offset, value in ((base, ids[at].astype(F32).astype(BF)), (base + top, probs[at])):
            tail = tail + dot(value, (ahead == offset).astype(F32).astype(BF), 0, 0)
        for peer in range(out.shape[0]):
            out[peer, :, m * width : (m + 1) * width] = rows[at]
    for peer in range(out.shape[0]):
        out[peer, :, mb * width :] = tail.astype(BF)


def route_maps(names, first, size, nq, toks, cap):
    tokens, top = names.shape
    shape = (tokens, size)
    column = iota(shape, 1)
    expert = (first + lax.div(column, nq)).astype(F32)
    same = lax.div(iota(shape, 0), toks) == lax.rem(column, nq)
    picks = [jnp.where(same & (names[:, k : k + 1] == expert), 1.0, 0.0) for k in range(top)]
    hits = functools.reduce(jnp.add, picks)
    lower = jnp.where(iota((tokens, tokens), 0) > iota((tokens, tokens), 1), 1.0, 0.0)
    slot = dot(lower.astype(BF), hits.astype(BF), 1, 0)
    return picks, [jnp.where(slot == s, hits, 0.0) for s in range(cap)]


def small_lines(lines, mb, top, width):
    tail = lines[:, mb * width :]
    shape = (PAD, PAD)
    parts = []
    for m in range(mb):
        move = (iota(shape, 0) == iota(shape, 1) + 2 * m * top).astype(F32).astype(BF)
        parts.append(dot(tail, move, 1, 0))
    return jnp.concatenate(parts, axis=0)


def pack_kernel(dims, first, lines, out):
    nd, nq, mb, toks, top, cap, width = dims
    tail_in = small_lines(lines, mb, top, width)
    picks, maps = route_maps(tail_in[:, :top], first[0], nd * nq, nq, toks, cap)
    grads = jnp.concatenate([lines[:, m * width : (m + 1) * width] for m in range(mb)], axis=0)
    tokens = grads.shape[0]
    held = functools.reduce(
        jnp.add, [k * tail_in[:, top + i : top + i + 1] for i, k in enumerate(picks)]
    )
    tail = jnp.zeros((nd * nq, PAD), F32)
    for s, k in enumerate(maps):
        out[:, s * width : (s + 1) * width] = dot(k.astype(BF), grads, 0, 0).astype(BF)
        lane = jnp.where(iota((tokens, PAD), 1) == s, 1.0, 0.0).astype(BF)
        tail = tail + dot((k * held).astype(BF), lane, 0, 0)
    out[:, cap * width :] = tail.astype(BF)


def unpack_kernel(dims, first, lines, home, out):
    nd, nq, mb, toks, top, cap, width = dims
    names = small_lines(lines, mb, top, width)[:, :top]
    picks, maps = route_maps(names, first[0], nd * nq, nq, toks, cap)
    tokens = names.shape[0]
    total = jnp.zeros((tokens, width), F32)
    held = jnp.zeros((tokens, nd * nq), F32)
    tail = home[:, cap * width :]
    for s, k in enumerate(maps):
        total = total + dot(k.astype(BF), home[:, s * width : (s + 1) * width], 1, 0)
        lane = jnp.where(iota((tokens, PAD), 1) == s, 1.0, 0.0).astype(BF)
        held = held + k * dot(lane, tail, 1, 1)
    run = tokens // mb
    lane = iota((run, PAD), 1)
    picked = jnp.zeros((run, PAD), F32)
    for m in range(mb):
        at = slice(m * run, (m + 1) * run)
        out[:, m * width : (m + 1) * width] = total[at].astype(BF)
        for i, k in enumerate(picks):
            value = jnp.sum(k[at] * held[at], axis=1, keepdims=True)
            picked = jnp.where(lane == m * top + i, value, picked)
    out[:, mb * width :] = picked.astype(BF)


def total_kernel(me, parts, in_grad, prob_grad):
    mb, toks, width = in_grad.shape
    top = prob_grad.shape[1]
    total = functools.reduce(jnp.add, [parts[i].astype(F32) for i in range(parts.shape[0])])
    tail = total[:, mb * width :].astype(BF)
    ahead = iota((top, PAD), 1) - iota((top, PAD), 0)
    for m in range(mb):
        in_grad[me[0] ^ m] = total[:, m * width : (m + 1) * width].astype(BF)
        column = (ahead == m * top).astype(F32).astype(BF)
        prob_grad[me[0] ^ m] = dot(column, tail, 1, 1).astype(BF)


def first_row(shape, nd, nq, mb, cap):
    column = iota(shape, 1)
    return (lax.rem(lax.rem(column, nq), nq // mb) * nd + lax.div(column, nq)) * cap


def spread(nd, nq, mb, cap, m, s=None):
    rows = (nd * nq // mb) * cap
    shape = (rows, nd * nq)
    ahead = iota(shape, 0) - first_row(shape, nd, nq, mb, cap)
    here = (ahead >= 0) & (ahead < cap) if s is None else ahead == s
    here = here & (lax.div(lax.rem(iota(shape, 1), nq), nq // mb) == m)
    return jnp.where(here, 1.0, 0.0).astype(BF)


def down_kernel(nd, nq, mb, cap, m, got, w_down, part, rows, probs):
    slots, width = rows.shape
    total = jnp.zeros((slots, width), F32)
    for s in range(cap):
        total = total + dot(
            spread(nd, nq, mb, cap, m, s), got[:, s * width : (s + 1) * width], 1, 0
        )
    mine = total.astype(BF)
    rows[...] = mine
    part[...] = dot(mine, w_down[...], 1, 1)
    tail = dot(spread(nd, nq, mb, cap, m), got[:, cap * width :], 1, 0)
    shape = (slots, PAD)
    probs[...] = jnp.sum(
        jnp.where(iota(shape, 1) == lax.rem(iota(shape, 0), cap), tail, 0.0), axis=1, keepdims=True
    )


def sum_kernel(mine, own, others, out):
    n = others.shape[0]
    total = functools.reduce(
        jnp.add, [jnp.where(mine[0] == i, own[i], others[i].astype(F32)) for i in range(n)]
    )
    out[...] = total.astype(BF)


def pair_kernel(first, second, out):
    total = (first[...].astype(F32) + second[...].astype(F32)).astype(BF)
    for i in range(out.shape[0]):
        out[i] = total


def act_kernel(me, gate, up, probs0, probs1, rows0, rows1, f_gate, f_up, hidden, grad):
    total = None
    for m, (probs, rows) in enumerate(((probs0, rows0), (probs1, rows1))):
        gate_f = gate[me[0] ^ m].astype(F32)
        up_f = up[me[0] ^ m].astype(F32)
        p = probs[...]
        sig = 1.0 / (1.0 + jnp.exp(-gate_f))
        act = gate_f * sig
        h = act * up_f
        f_gate[m] = p * up_f * (sig * (1.0 + gate_f * (1.0 - sig)))
        f_up[m] = p * act
        hidden[m] = h
        term = dot((p * h).astype(BF), rows[...], 0, 0)
        total = term if total is None else total + term
    grad[...] = total.astype(BF)


def slot_kernel(nd, nq, mb, cap, m, u_ref, f_gate, f_up, hidden, w_gate, w_up, *rest):
    before, (dgate, dup, out) = rest[:-3], rest[-3:]
    u = u_ref[...].astype(F32)
    dg = (u * f_gate[m]).astype(BF)
    du = (u * f_up[m]).astype(BF)
    dgate[...] = dg
    dup[...] = du
    rows = (dot(dg, w_gate[...], 1, 1) + dot(du, w_up[...], 1, 1)).astype(BF)
    slots, width = rows.shape

    def put(low, high, value):
        if before:
            value = value + before[0][:, low:high].astype(F32)
        out[:, low:high] = value.astype(BF)

    for s in range(cap):
        put(s * width, (s + 1) * width, dot(spread(nd, nq, mb, cap, m, s), rows, 0, 0))
    slot_prob = jnp.sum(u * hidden[m], axis=1, keepdims=True)
    shape = (slots, PAD)
    tail = jnp.where(iota(shape, 1) == lax.rem(iota(shape, 0), cap), slot_prob, 0.0).astype(BF)
    put(cap * width, cap * width + PAD, dot(spread(nd, nq, mb, cap, m), tail, 0, 0))


def weight_kernel(me, inputs, dgate0, dup0, dgate1, dup1, grad_gate, grad_up):
    first, second = inputs[me[0]], inputs[me[0] ^ 1]
    grad_gate[...] = (dot(first, dgate0[...], 0, 0) + dot(second, dgate1[...], 0, 0)).astype(BF)
    grad_up[...] = (dot(first, dup0[...], 0, 0) + dot(second, dup1[...], 0, 0)).astype(BF)


def local(out_grad, expert_ids, probs, saved_inputs, gate_pre, up_pre, w_gate, w_up, w_down):
    sds = jax.ShapeDtypeStruct
    ne = lax.axis_size(EX)
    n_x = lax.axis_size("x")
    mb, toks, top = expert_ids.shape
    slots = saved_inputs.shape[2]
    cap = slots // ne
    width = out_grad.shape[2]
    ff = w_gate.shape[2]
    line = cap * width + PAD
    w_gate, w_up, w_down = w_gate[0], w_up[0], w_down[0]
    core = lax.axis_index("core")
    me = core.astype(jnp.int32).reshape(1)
    product = 2 * slots * width * ff

    n_a, nd = lax.axis_size("za"), lax.axis_size(PLANE)
    nq = n_a * mb
    dims = (nd, nq, mb, toks, top, cap, width)
    wide = mb * width + PAD
    first = (lax.axis_index("za").astype(jnp.int32) * nd).reshape(1)

    hbm = pl.BlockSpec(memory_space=pltpu.HBM)
    flat = pl.pallas_call(
        flat_kernel,
        out_shape=sds((n_a, toks, wide), BF),
        in_specs=[SMEM, hbm, hbm, hbm],
        out_specs=VMEM,
        scratch_shapes=[
            pltpu.VMEM((mb, top, toks), jnp.int32),
            pltpu.VMEM((mb, top, toks), BF),
            pltpu.VMEM((mb, toks, width), BF),
            pltpu.SemaphoreType.DMA((3,)),
        ],
        compiler_params=pltpu.CompilerParams(vmem_limit_bytes=56 << 20),
    )(me, jnp.swapaxes(expert_ids, 1, 2), jnp.swapaxes(probs, 1, 2), out_grad)
    lines = lax.all_to_all(flat, "za", 0, 0, tiled=True).reshape(n_a * toks, wide)
    send = call(
        functools.partial(pack_kernel, dims), [sds((nd * nq, line), BF)], 1, 16 * product, nd * nq * line * 64
    )(first, lines)[0]
    got = lax.all_to_all(send.reshape(nd, nq, line), PLANE, 0, 0, tiled=True).reshape(nd * nq, line)

    def down(m):
        return call(
            functools.partial(down_kernel, nd, nq, mb, cap, m),
            [sds((slots, ff), F32), sds((slots, width), BF), sds((slots, 1), F32)],
            2,
            product,
            slots * ff * 4,
            has_me=False,
        )(got, w_down)

    part1, rows1, probs1 = down(1)
    away = lax.ppermute(part1, "core", SWAP)
    part0, rows0, probs0 = down(0)
    half = (part0 + away).reshape(n_x, slots // n_x, ff)
    others = lax.all_to_all(half.astype(BF), "x", 0, 0, tiled=True)
    mine = lax.axis_index("x").astype(jnp.int32).reshape(1)
    piece = (slots // n_x, ff)
    eighth = call(
        sum_kernel, [sds(piece, BF)], 2, 0, slots * ff * 6
    )(mine, half, others)[0]
    other = lax.ppermute(eighth, "zh", SWAP)

    f_gate, f_up, hidden, grad_down = call(
        act_kernel,
        [sds((mb, slots, ff), F32)] * 3 + [sds((ff, width), BF)],
        6,
        2 * product,
        mb * slots * ff * 16,
        limit=32,
    )(me, gate_pre[:, 0], up_pre[:, 0], probs0, probs1, rows0, rows1)

    other, f_gate, f_up, hidden = lax.optimization_barrier((other, f_gate, f_up, hidden))
    u = call(
        pair_kernel, [sds((n_x,) + piece, BF)], 2, 0, slots * ff * 2, has_me=False
    )(eighth, other)[0]
    u0 = lax.all_to_all(u, "x", 0, 0, tiled=True).reshape(slots, ff)
    u1 = lax.ppermute(u0, "core", SWAP)

    def slot(m, u_m, *before):
        return call(
            functools.partial(slot_kernel, nd, nq, mb, cap, m),
            [sds((slots, ff), BF), sds((slots, ff), BF), sds((nd * nq, line), BF)],
            6 + len(before),
            2 * product,
            slots * ff * 16,
            has_me=False,
        )(u_m, f_gate, f_up, hidden, w_gate, w_up, *before)

    dgate0, dup0, back = slot(0, u0)
    dgate1, dup1, back = slot(1, u1, back)
    home = lax.all_to_all(back.reshape(nd, nq, line), PLANE, 0, 0, tiled=True)
    part = call(
        functools.partial(unpack_kernel, dims),
        [sds((n_a * toks, wide), BF)],
        2,
        product // 4,
        nd * nq * line * 2,
    )(first, lines, home.reshape(nd * nq, line))[0]
    part = lax.all_to_all(part.reshape(n_a, toks, wide), "za", 0, 0, tiled=True)
    grad_gate, grad_up = call(
        weight_kernel, [sds((width, ff), BF)] * 2, 5, 4 * product, slots * ff * 12
    )(me, saved_inputs[:, 0], dgate0, dup0, dgate1, dup1)
    in_grad, prob_grad = call(
        total_kernel,
        [sds((mb, toks, width), BF), sds((mb, top, toks), BF)],
        1,
        0,
        toks * width * 20,
    )(me, part)
    prob_grad = jnp.swapaxes(prob_grad, 1, 2)
    return in_grad, prob_grad, grad_gate[None], grad_up[None], grad_down[None]


def solution(mesh):
    n_dp, n_ex = mesh.devices.shape
    n_a = 4 if n_ex >= 64 else 2
    fine = Mesh(
        mesh.devices.reshape(2, n_dp // 4, 2, n_a, n_ex // (4 * n_a), 4),
        ("zh", "x", "core", "za", "zb", "y"),
    )
    specs = (
        P(None, EX, DP),
        P(None, EX, None),
        P(None, EX, None),
        P(None, EX, None, DP),
        P(None, EX, None, None),
        P(None, EX, None, None),
        P(EX, DP, None),
        P(EX, DP, None),
        P(EX, None, DP),
    )
    return jax.shard_map(
        local,
        mesh=fine,
        in_specs=specs,
        out_specs=(specs[0], specs[1], specs[6], specs[7], specs[8]),
        check_vma=False,
    )
```

```python
import functools

import jax
import jax.numpy as jnp
from jax import lax
from jax.experimental import pallas as pl
from jax.experimental.pallas import tpu as pltpu
from jax.sharding import Mesh
from jax.sharding import PartitionSpec as P

BF = jnp.bfloat16
F32 = jnp.float32
DP = ("zh", "x", "core")
EX = ("za", "zb", "y")
PLANE = ("zb", "y")
PAD = 128
SWAP = [(0, 1), (1, 0)]
VMEM = pl.BlockSpec(memory_space=pltpu.VMEM)
SMEM = pl.BlockSpec(memory_space=pltpu.SMEM)


def dot(a, b, ca, cb):
    return lax.dot_general(a, b, (((ca,), (cb,)), ((), ())), preferred_element_type=F32)


def iota(shape, dim):
    return lax.broadcasted_iota(jnp.int32, shape, dim)


def call(body, outs, n_in, flops, bytes_moved, limit=24, has_me=True):
    first = [SMEM] if has_me else []
    return pl.pallas_call(
        body,
        out_shape=outs,
        in_specs=first + [VMEM] * n_in,
        out_specs=[VMEM] * len(outs),
        cost_estimate=pl.CostEstimate(flops=flops, bytes_accessed=bytes_moved, transcendentals=0),
        compiler_params=pltpu.CompilerParams(vmem_limit_bytes=limit << 20),
    )


def flat_kernel(ids_in, probs_in, rows_in, out, ids, probs, rows, sems):
    copies = [
        pltpu.make_async_copy(source, held, sems.at[i])
        for i, (source, held) in enumerate(((ids_in, ids), (probs_in, probs), (rows_in, rows)))
    ]
    for copy in copies:
        copy.start()
    for copy in copies:
        copy.wait()
    mb, toks, width = rows.shape
    top = ids.shape[1]
    peers = out.shape[0] // mb
    ahead = iota((top, PAD), 1) - iota((top, PAD), 0)
    for m in range(mb):
        tail = dot(ids[m].astype(F32).astype(BF), (ahead == 0).astype(F32).astype(BF), 0, 0)
        tail = tail + dot(probs[m], (ahead == top).astype(F32).astype(BF), 0, 0)
        for peer in range(m * peers, (m + 1) * peers):
            out[peer, :, :width] = rows[m]
            out[peer, :, width:] = tail.astype(BF)


def route_maps(names, first, size, nq, toks, cap):
    tokens, top = names.shape
    shape = (tokens, size)
    column = iota(shape, 1)
    expert = (first + lax.div(column, nq)).astype(F32)
    same = lax.div(iota(shape, 0), toks) == lax.rem(column, nq)
    picks = [jnp.where(same & (names[:, k : k + 1] == expert), 1.0, 0.0) for k in range(top)]
    hits = functools.reduce(jnp.add, picks)
    lower = jnp.where(iota((tokens, tokens), 0) > iota((tokens, tokens), 1), 1.0, 0.0)
    slot = dot(lower.astype(BF), hits.astype(BF), 1, 0)
    return picks, [jnp.where(slot == s, hits, 0.0) for s in range(cap)]


def pack_kernel(dims, first, lines, out):
    nd, nq, toks, top, cap, width = dims
    tail_in = lines[:, width:].astype(F32)
    picks, maps = route_maps(tail_in[:, :top], first[0], nd * nq, nq, toks, cap)
    grads = lines[:, :width]
    tokens = grads.shape[0]
    held = functools.reduce(
        jnp.add, [k * tail_in[:, top + i : top + i + 1] for i, k in enumerate(picks)]
    )
    tail = jnp.zeros((nd * nq, PAD), F32)
    for s, k in enumerate(maps):
        out[:, s * width : (s + 1) * width] = dot(k.astype(BF), grads, 0, 0).astype(BF)
        lane = jnp.where(iota((tokens, PAD), 1) == s, 1.0, 0.0).astype(BF)
        tail = tail + dot((k * held).astype(BF), lane, 0, 0)
    out[:, cap * width :] = tail.astype(BF)


def unpack_kernel(dims, first, lines, home, out):
    nd, nq, toks, top, cap, width = dims
    names = lines[:, width:].astype(F32)[:, :top]
    picks, maps = route_maps(names, first[0], nd * nq, nq, toks, cap)
    tokens = names.shape[0]
    total = jnp.zeros((tokens, width), F32)
    held = jnp.zeros((tokens, nd * nq), F32)
    tail = home[:, cap * width :]
    for s, k in enumerate(maps):
        total = total + dot(k.astype(BF), home[:, s * width : (s + 1) * width], 1, 0)
        lane = jnp.where(iota((tokens, PAD), 1) == s, 1.0, 0.0).astype(BF)
        held = held + k * dot(lane, tail, 1, 1)
    out[:, :width] = total.astype(BF)
    lane = iota((tokens, PAD), 1)
    picked = jnp.zeros((tokens, PAD), F32)
    for i, k in enumerate(picks):
        picked = jnp.where(lane == i, jnp.sum(k * held, axis=1, keepdims=True), picked)
    out[:, width:] = picked.astype(BF)


def total_kernel(parts, in_grad, prob_grad):
    mb, toks, width = in_grad.shape
    top = prob_grad.shape[1]
    n = parts.shape[0] // mb
    column = (iota((top, PAD), 1) == iota((top, PAD), 0)).astype(F32).astype(BF)
    for m in range(mb):
        total = functools.reduce(
            jnp.add, [parts[i].astype(F32) for i in range(m * n, (m + 1) * n)]
        )
        in_grad[m] = total[:, :width].astype(BF)
        prob_grad[m] = dot(column, total[:, width:].astype(BF), 1, 1).astype(BF)


def first_row(shape, nd, nq, mb, cap):
    column = iota(shape, 1)
    return (lax.rem(lax.rem(column, nq), nq // mb) * nd + lax.div(column, nq)) * cap


def spread(nd, nq, mb, cap, m, s=None):
    rows = (nd * nq // mb) * cap
    shape = (rows, nd * nq)
    ahead = iota(shape, 0) - first_row(shape, nd, nq, mb, cap)
    here = (ahead >= 0) & (ahead < cap) if s is None else ahead == s
    here = here & (lax.div(lax.rem(iota(shape, 1), nq), nq // mb) == m)
    return jnp.where(here, 1.0, 0.0).astype(BF)


def down_kernel(nd, nq, nb, cap, me, got, w_mine, w_other, part, half, mine, other, probs):
    slots, width = mine.shape
    blocks = []
    for d in range(nb):
        total = jnp.zeros((slots, width), F32)
        for s in range(cap):
            total = total + dot(
                spread(nd, nq, nb, cap, d, s), got[:, s * width : (s + 1) * width], 1, 0
            )
        blocks.append(total)
    own = jnp.where(me[0] == 0, blocks[0], blocks[1]).astype(BF)
    far = jnp.where(me[0] == 0, blocks[1], blocks[0]).astype(BF)
    mine[...] = own
    other[...] = far
    total = dot(own, w_mine[...], 1, 1) + dot(far, w_other[...], 1, 1)
    part[...] = total
    half[...] = total.astype(BF)
    tail = dot(spread(nd, nq, nb, cap, 0), got[:, cap * width :], 1, 0)
    shape = (slots, PAD)
    probs[...] = jnp.sum(
        jnp.where(iota(shape, 1) == lax.rem(iota(shape, 0), cap), tail, 0.0), axis=1, keepdims=True
    )


def sum_kernel(mine, own, others, out):
    n = others.shape[0]
    total = functools.reduce(
        jnp.add, [jnp.where(mine[0] == i, own[i], others[i].astype(F32)) for i in range(n)]
    )
    out[...] = total.astype(BF)


def pair_kernel(first, second, out):
    total = (first[...].astype(F32) + second[...].astype(F32)).astype(BF)
    for i in range(out.shape[0]):
        out[i] = total


def act_kernel(me, gate, up, probs, f_gate, f_up, hidden):
    gate_f = gate[me[0]].astype(F32)
    up_f = up[me[0]].astype(F32)
    p = probs[...]
    sig = 1.0 / (1.0 + jnp.exp(-gate_f))
    act = gate_f * sig
    f_gate[...] = p * up_f * (sig * (1.0 + gate_f * (1.0 - sig)))
    f_up[...] = p * act
    hidden[...] = act * up_f


def down_grad_kernel(me, gate, up, probs0, probs1, rows0, rows1, grad):
    total = None
    for m, (probs, rows) in enumerate(((probs0, rows0), (probs1, rows1))):
        gate_f = gate[me[0] ^ m].astype(F32)
        act = gate_f * (1.0 / (1.0 + jnp.exp(-gate_f)))
        scaled = (probs[...] * (act * up[me[0] ^ m].astype(F32))).astype(BF)
        term = dot(scaled, rows[...], 0, 0)
        total = term if total is None else total + term
    grad[...] = total.astype(BF)


def slot_kernel(nd, nq, nb, cap, me, u_ref, f_gate, f_up, hidden, wg, wu, wg_far, wu_far, grads, out):
    u = u_ref[...].astype(F32)
    dg = (u * f_gate[...]).astype(BF)
    du = (u * f_up[...]).astype(BF)
    grads[0] = dg
    grads[1] = du
    own = dot(dg, wg[...], 1, 1) + dot(du, wu[...], 1, 1)
    far = dot(dg, wg_far[...], 1, 1) + dot(du, wu_far[...], 1, 1)
    blocks = [
        jnp.where(me[0] == 0, own, far).astype(BF),
        jnp.where(me[0] == 0, far, own).astype(BF),
    ]
    slots, width = blocks[0].shape
    for s in range(cap):
        lines = functools.reduce(
            jnp.add, [dot(spread(nd, nq, nb, cap, d, s), blocks[d], 0, 0) for d in range(nb)]
        )
        out[:, s * width : (s + 1) * width] = lines.astype(BF)
    slot_prob = jnp.sum(u * hidden[...], axis=1, keepdims=True)
    shape = (slots, PAD)
    tail = jnp.where(iota(shape, 1) == lax.rem(iota(shape, 0), cap), slot_prob, 0.0).astype(BF)
    tails = functools.reduce(
        jnp.add, [dot(spread(nd, nq, nb, cap, d), tail, 0, 0) for d in range(nb)]
    )
    out[:, cap * width :] = tails.astype(BF)


def weight_kernel(me, inputs, grads0, grads1, grad_gate, grad_up):
    first, second = inputs[me[0]], inputs[me[0] ^ 1]
    for i, out in enumerate((grad_gate, grad_up)):
        out[...] = (dot(first, grads0[i], 0, 0) + dot(second, grads1[i], 0, 0)).astype(BF)


def local(out_grad, expert_ids, probs, saved_inputs, gate_pre, up_pre, w_gate, w_up, w_down):
    sds = jax.ShapeDtypeStruct
    ne = lax.axis_size(EX)
    n_x = lax.axis_size("x")
    mb, toks, top = expert_ids.shape
    slots = saved_inputs.shape[2]
    cap = slots // ne
    width = out_grad.shape[2]
    ff = w_gate.shape[2]
    line = cap * width + PAD
    w_gate, w_up, w_down = w_gate[0], w_up[0], w_down[0]
    core = lax.axis_index("core")
    me = core.astype(jnp.int32).reshape(1)
    product = 2 * slots * width * ff

    n_a, nd = lax.axis_size("za"), lax.axis_size(PLANE)
    nb = mb
    nq = n_a * nb
    dims = (nd, nq, toks, top, cap, width)
    wide = width + PAD
    first = (lax.axis_index("za").astype(jnp.int32) * nd).reshape(1)

    hbm = pl.BlockSpec(memory_space=pltpu.HBM)
    flat = pl.pallas_call(
        flat_kernel,
        out_shape=sds((nq, toks, wide), BF),
        in_specs=[hbm, hbm, hbm],
        out_specs=VMEM,
        scratch_shapes=[
            pltpu.VMEM((mb, top, toks), jnp.int32),
            pltpu.VMEM((mb, top, toks), BF),
            pltpu.VMEM((mb, toks, width), BF),
            pltpu.SemaphoreType.DMA((3,)),
        ],
        compiler_params=pltpu.CompilerParams(vmem_limit_bytes=56 << 20),
    )(jnp.swapaxes(expert_ids, 1, 2), jnp.swapaxes(probs, 1, 2), out_grad)
    flat, w_down = lax.optimization_barrier((flat, w_down))
    w_far = lax.ppermute(w_down, "core", SWAP)
    lines = lax.all_to_all(flat, ("core", "za"), 0, 0, tiled=True).reshape(nq * toks, wide)
    send = call(
        functools.partial(pack_kernel, dims), [sds((nd * nq, line), BF)], 1, 16 * product, nd * nq * line * 64
    )(first, lines)[0]
    got = lax.all_to_all(send.reshape(nd, nq, line), PLANE, 0, 0, tiled=True).reshape(nd * nq, line)
    part, half, rows0, rows_far, probs0 = call(
        functools.partial(down_kernel, nd, nq, nb, cap),
        [
            sds((slots, ff), F32),
            sds((slots, ff), BF),
            sds((slots, width), BF),
            sds((slots, width), BF),
            sds((slots, 1), F32),
        ],
        3,
        2 * product,
        slots * ff * 6,
    )(me, got, w_down, w_far)
    half = half.reshape(n_x, slots // n_x, ff)
    part = part.reshape(n_x, slots // n_x, ff)
    others = lax.all_to_all(half, "x", 0, 0, tiled=True)
    mine = lax.axis_index("x").astype(jnp.int32).reshape(1)
    piece = (slots // n_x, ff)
    eighth = call(
        sum_kernel, [sds(piece, BF)], 2, 0, slots * ff * 6
    )(mine, part, others)[0]
    other = lax.ppermute(eighth, "zh", SWAP)

    probs_later, _ = lax.optimization_barrier((probs0, eighth))
    f_gate, f_up, hidden = call(
        act_kernel, [sds((slots, ff), F32)] * 3, 3, slots * ff * 20, slots * ff * 16
    )(me, gate_pre[:, 0], up_pre[:, 0], probs_later)
    f_gate, w_gate_now, w_up_now, rows_far, probs_now = lax.optimization_barrier(
        (f_gate, w_gate, w_up, rows_far, probs0)
    )
    wg_far = lax.ppermute(w_gate_now, "core", SWAP)
    wu_far = lax.ppermute(w_up_now, "core", SWAP)
    rows1 = lax.ppermute(rows_far, "core", SWAP)
    probs1 = lax.ppermute(probs_now, "core", SWAP)
    grad_down = call(
        down_grad_kernel, [sds((ff, width), BF)], 6, 2 * product, slots * ff * 12
    )(me, gate_pre[:, 0], up_pre[:, 0], probs0, probs1, rows0, rows1)[0]

    other, f_gate, f_up, hidden, wg_far, wu_far, grad_down = lax.optimization_barrier(
        (other, f_gate, f_up, hidden, wg_far, wu_far, grad_down)
    )
    u = call(
        pair_kernel, [sds((n_x,) + piece, BF)], 2, 0, slots * ff * 2, has_me=False
    )(eighth, other)[0]
    u0 = lax.all_to_all(u, "x", 0, 0, tiled=True).reshape(slots, ff)
    grads0, back = call(
        functools.partial(slot_kernel, nd, nq, nb, cap),
        [sds((2, slots, ff), BF), sds((nd * nq, line), BF)],
        8,
        4 * product,
        slots * ff * 24,
    )(me, u0, f_gate, f_up, hidden, w_gate, w_up, wg_far, wu_far)
    home = lax.all_to_all(back.reshape(nd, nq, line), PLANE, 0, 0, tiled=True)
    part = call(
        functools.partial(unpack_kernel, dims),
        [sds((nq * toks, wide), BF)],
        2,
        product // 4,
        nd * nq * line * 2,
    )(first, lines, home.reshape(nd * nq, line))[0]
    grads1 = lax.ppermute(grads0, "core", SWAP)
    part = lax.all_to_all(part.reshape(nq, toks, wide), ("core", "za"), 0, 0, tiled=True)
    grad_gate, grad_up = call(
        weight_kernel, [sds((width, ff), BF)] * 2, 3, 4 * product, slots * ff * 12
    )(me, saved_inputs[:, 0], grads0, grads1)
    in_grad, prob_grad = call(
        total_kernel,
        [sds((mb, toks, width), BF), sds((mb, top, toks), BF)],
        1,
        0,
        toks * width * 20,
        has_me=False,
    )(part)
    prob_grad = jnp.swapaxes(prob_grad, 1, 2)
    return in_grad, prob_grad, grad_gate[None], grad_up[None], grad_down[None]


def solution(mesh):
    n_dp, n_ex = mesh.devices.shape
    n_a = 4 if n_ex >= 64 else 2
    fine = Mesh(
        mesh.devices.reshape(2, n_dp // 4, 2, n_a, n_ex // (4 * n_a), 4),
        ("zh", "x", "core", "za", "zb", "y"),
    )
    specs = (
        P(None, EX, DP),
        P(None, EX, None),
        P(None, EX, None),
        P(None, EX, None, DP),
        P(None, EX, None, None),
        P(None, EX, None, None),
        P(EX, DP, None),
        P(EX, DP, None),
        P(EX, None, DP),
    )
    return jax.shard_map(
        local,
        mesh=fine,
        in_specs=specs,
        out_specs=(specs[0], specs[1], specs[6], specs[7], specs[8]),
        check_vma=False,
    )
```

```python
import functools

import jax
import jax.numpy as jnp
from jax import lax
from jax.experimental import pallas as pl
from jax.experimental.pallas import tpu as pltpu
from jax.sharding import Mesh
from jax.sharding import PartitionSpec as P

BF = jnp.bfloat16
F32 = jnp.float32
DP = ("zh", "x", "core")
EX = ("za", "zb", "y")
PLANE = ("zb", "y")
PAD = 128
SWAP = [(0, 1), (1, 0)]
VMEM = pl.BlockSpec(memory_space=pltpu.VMEM)
SMEM = pl.BlockSpec(memory_space=pltpu.SMEM)


def dot(a, b, ca, cb):
    return lax.dot_general(a, b, (((ca,), (cb,)), ((), ())), preferred_element_type=F32)


def iota(shape, dim):
    return lax.broadcasted_iota(jnp.int32, shape, dim)


def call(body, outs, n_in, flops, bytes_moved, limit=24, has_me=True):
    first = [SMEM] if has_me else []
    return pl.pallas_call(
        body,
        out_shape=outs,
        in_specs=first + [VMEM] * n_in,
        out_specs=[VMEM] * len(outs),
        cost_estimate=pl.CostEstimate(flops=flops, bytes_accessed=bytes_moved, transcendentals=0),
        compiler_params=pltpu.CompilerParams(vmem_limit_bytes=limit << 20),
    )


def flat_kernel(ids_in, probs_in, rows_in, out, ids, probs, rows, sems):
    copies = [
        pltpu.make_async_copy(source, held, sems.at[i])
        for i, (source, held) in enumerate(((ids_in, ids), (probs_in, probs), (rows_in, rows)))
    ]
    for copy in copies:
        copy.start()
    for copy in copies:
        copy.wait()
    mb, toks, width = rows.shape
    top = ids.shape[1]
    peers = out.shape[0] // mb
    ahead = iota((top, PAD), 1) - iota((top, PAD), 0)
    for m in range(mb):
        tail = dot(ids[m].astype(F32).astype(BF), (ahead == 0).astype(F32).astype(BF), 0, 0)
        tail = tail + dot(probs[m], (ahead == top).astype(F32).astype(BF), 0, 0)
        for peer in range(m * peers, (m + 1) * peers):
            out[peer, :, :width] = rows[m]
            out[peer, :, width:] = tail.astype(BF)


def route_maps(names, first, size, nq, toks, cap):
    tokens, top = names.shape
    shape = (tokens, size)
    column = iota(shape, 1)
    expert = (first + lax.div(column, nq)).astype(F32)
    same = lax.div(iota(shape, 0), toks) == lax.rem(column, nq)
    picks = [jnp.where(same & (names[:, k : k + 1] == expert), 1.0, 0.0) for k in range(top)]
    hits = functools.reduce(jnp.add, picks)
    lower = jnp.where(iota((tokens, tokens), 0) > iota((tokens, tokens), 1), 1.0, 0.0)
    slot = dot(lower.astype(BF), hits.astype(BF), 1, 0)
    return picks, [jnp.where(slot == s, hits, 0.0) for s in range(cap)]


def pack_kernel(dims, first, lines, out):
    nd, nq, toks, top, cap, width = dims
    tail_in = lines[:, width:].astype(F32)
    picks, maps = route_maps(tail_in[:, :top], first[0], nd * nq, nq, toks, cap)
    grads = lines[:, :width]
    tokens = grads.shape[0]
    held = functools.reduce(
        jnp.add, [k * tail_in[:, top + i : top + i + 1] for i, k in enumerate(picks)]
    )
    tail = jnp.zeros((nd * nq, PAD), F32)
    for s, k in enumerate(maps):
        out[:, s * width : (s + 1) * width] = dot(k.astype(BF), grads, 0, 0).astype(BF)
        lane = jnp.where(iota((tokens, PAD), 1) == s, 1.0, 0.0).astype(BF)
        tail = tail + dot((k * held).astype(BF), lane, 0, 0)
    out[:, cap * width :] = tail.astype(BF)


def unpack_kernel(dims, first, lines, home, out):
    nd, nq, toks, top, cap, width = dims
    names = lines[:, width:].astype(F32)[:, :top]
    picks, maps = route_maps(names, first[0], nd * nq, nq, toks, cap)
    tokens = names.shape[0]
    total = jnp.zeros((tokens, width), F32)
    held = jnp.zeros((tokens, nd * nq), F32)
    tail = home[:, cap * width :]
    for s, k in enumerate(maps):
        total = total + dot(k.astype(BF), home[:, s * width : (s + 1) * width], 1, 0)
        lane = jnp.where(iota((tokens, PAD), 1) == s, 1.0, 0.0).astype(BF)
        held = held + k * dot(lane, tail, 1, 1)
    out[:, :width] = total.astype(BF)
    lane = iota((tokens, PAD), 1)
    picked = jnp.zeros((tokens, PAD), F32)
    for i, k in enumerate(picks):
        picked = jnp.where(lane == i, jnp.sum(k * held, axis=1, keepdims=True), picked)
    out[:, width:] = picked.astype(BF)


def total_kernel(parts, in_grad, prob_grad):
    mb, toks, width = in_grad.shape
    top = prob_grad.shape[1]
    n = parts.shape[0] // mb
    column = (iota((top, PAD), 1) == iota((top, PAD), 0)).astype(F32).astype(BF)
    for m in range(mb):
        total = functools.reduce(
            jnp.add, [parts[i].astype(F32) for i in range(m * n, (m + 1) * n)]
        )
        in_grad[m] = total[:, :width].astype(BF)
        prob_grad[m] = dot(column, total[:, width:].astype(BF), 1, 1).astype(BF)


def first_row(shape, nd, nq, mb, cap):
    column = iota(shape, 1)
    return (lax.rem(lax.rem(column, nq), nq // mb) * nd + lax.div(column, nq)) * cap


def spread(nd, nq, mb, cap, m, s=None):
    rows = (nd * nq // mb) * cap
    shape = (rows, nd * nq)
    ahead = iota(shape, 0) - first_row(shape, nd, nq, mb, cap)
    here = (ahead >= 0) & (ahead < cap) if s is None else ahead == s
    here = here & (lax.div(lax.rem(iota(shape, 1), nq), nq // mb) == m)
    return jnp.where(here, 1.0, 0.0).astype(BF)


def down_kernel(nd, nq, nb, cap, me, got, w_mine, w_other, part, half, mine, other, probs):
    slots, width = mine.shape
    blocks = []
    for d in range(nb):
        total = jnp.zeros((slots, width), F32)
        for s in range(cap):
            total = total + dot(
                spread(nd, nq, nb, cap, d, s), got[:, s * width : (s + 1) * width], 1, 0
            )
        blocks.append(total)
    own = jnp.where(me[0] == 0, blocks[0], blocks[1]).astype(BF)
    far = jnp.where(me[0] == 0, blocks[1], blocks[0]).astype(BF)
    mine[...] = own
    other[...] = far
    total = dot(own, w_mine[...], 1, 1) + dot(far, w_other[...], 1, 1)
    part[...] = total
    half[...] = total.astype(BF)
    tail = dot(spread(nd, nq, nb, cap, 0), got[:, cap * width :], 1, 0)
    shape = (slots, PAD)
    probs[...] = jnp.sum(
        jnp.where(iota(shape, 1) == lax.rem(iota(shape, 0), cap), tail, 0.0), axis=1, keepdims=True
    )


def sum_kernel(mine, own, others, out):
    n = others.shape[0]
    total = functools.reduce(
        jnp.add, [jnp.where(mine[0] == i, own[i], others[i].astype(F32)) for i in range(n)]
    )
    out[...] = total.astype(BF)


def pair_kernel(first, second, out):
    total = (first[...].astype(F32) + second[...].astype(F32)).astype(BF)
    for i in range(out.shape[0]):
        out[i] = total


def act_kernel(me, gate, up, probs, f_gate, f_up, hidden):
    gate_f = gate[me[0]].astype(F32)
    up_f = up[me[0]].astype(F32)
    p = probs[...]
    sig = 1.0 / (1.0 + jnp.exp(-gate_f))
    act = gate_f * sig
    f_gate[...] = p * up_f * (sig * (1.0 + gate_f * (1.0 - sig)))
    f_up[...] = p * act
    hidden[...] = act * up_f


def down_grad_kernel(me, gate, up, probs0, probs1, rows0, rows1, grad):
    total = None
    for m, (probs, rows) in enumerate(((probs0, rows0), (probs1, rows1))):
        gate_f = gate[me[0] ^ m].astype(F32)
        act = gate_f * (1.0 / (1.0 + jnp.exp(-gate_f)))
        scaled = (probs[...] * (act * up[me[0] ^ m].astype(F32))).astype(BF)
        term = dot(scaled, rows[...], 0, 0)
        total = term if total is None else total + term
    grad[...] = total.astype(BF)


def slot_kernel(nd, nq, nb, cap, me, u_ref, f_gate, f_up, hidden, wg, wu, wg_far, wu_far, grads, out):
    u = u_ref[...].astype(F32)
    dg = (u * f_gate[...]).astype(BF)
    du = (u * f_up[...]).astype(BF)
    grads[0] = dg
    grads[1] = du
    own = dot(dg, wg[...], 1, 1) + dot(du, wu[...], 1, 1)
    far = dot(dg, wg_far[...], 1, 1) + dot(du, wu_far[...], 1, 1)
    blocks = [
        jnp.where(me[0] == 0, own, far).astype(BF),
        jnp.where(me[0] == 0, far, own).astype(BF),
    ]
    slots, width = blocks[0].shape
    for s in range(cap):
        lines = functools.reduce(
            jnp.add, [dot(spread(nd, nq, nb, cap, d, s), blocks[d], 0, 0) for d in range(nb)]
        )
        out[:, s * width : (s + 1) * width] = lines.astype(BF)
    slot_prob = jnp.sum(u * hidden[...], axis=1, keepdims=True)
    shape = (slots, PAD)
    tail = jnp.where(iota(shape, 1) == lax.rem(iota(shape, 0), cap), slot_prob, 0.0).astype(BF)
    tails = functools.reduce(
        jnp.add, [dot(spread(nd, nq, nb, cap, d), tail, 0, 0) for d in range(nb)]
    )
    out[:, cap * width :] = tails.astype(BF)


def weight_kernel(me, inputs, grads0, grads1, grad_gate, grad_up):
    first, second = inputs[me[0]], inputs[me[0] ^ 1]
    for i, out in enumerate((grad_gate, grad_up)):
        out[...] = (dot(first, grads0[i], 0, 0) + dot(second, grads1[i], 0, 0)).astype(BF)


def local(out_grad, expert_ids, probs, saved_inputs, gate_pre, up_pre, w_gate, w_up, w_down):
    sds = jax.ShapeDtypeStruct
    ne = lax.axis_size(EX)
    n_x = lax.axis_size("x")
    mb, toks, top = expert_ids.shape
    slots = saved_inputs.shape[2]
    cap = slots // ne
    width = out_grad.shape[2]
    ff = w_gate.shape[2]
    line = cap * width + PAD
    w_gate, w_up, w_down = w_gate[0], w_up[0], w_down[0]
    core = lax.axis_index("core")
    me = core.astype(jnp.int32).reshape(1)
    product = 2 * slots * width * ff

    n_a, nd = lax.axis_size("za"), lax.axis_size(PLANE)
    nb = mb
    nq = n_a * nb
    dims = (nd, nq, toks, top, cap, width)
    wide = width + PAD
    first = (lax.axis_index("za").astype(jnp.int32) * nd).reshape(1)

    hbm = pl.BlockSpec(memory_space=pltpu.HBM)
    flat = pl.pallas_call(
        flat_kernel,
        out_shape=sds((nq, toks, wide), BF),
        in_specs=[hbm, hbm, hbm],
        out_specs=VMEM,
        scratch_shapes=[
            pltpu.VMEM((mb, top, toks), jnp.int32),
            pltpu.VMEM((mb, top, toks), BF),
            pltpu.VMEM((mb, toks, width), BF),
            pltpu.SemaphoreType.DMA((3,)),
        ],
        compiler_params=pltpu.CompilerParams(vmem_limit_bytes=56 << 20),
    )(jnp.swapaxes(expert_ids, 1, 2), jnp.swapaxes(probs, 1, 2), out_grad)
    flat, *sent = lax.optimization_barrier((flat, w_down, w_gate, w_up))
    w_far, wg_far, wu_far = [lax.ppermute(w, "core", SWAP) for w in sent]
    lines = lax.all_to_all(flat, ("core", "za"), 0, 0, tiled=True).reshape(nq * toks, wide)
    lines, w_far, wg_far, wu_far = lax.optimization_barrier((lines, w_far, wg_far, wu_far))
    send = call(
        functools.partial(pack_kernel, dims), [sds((nd * nq, line), BF)], 1, 16 * product, nd * nq * line * 64
    )(first, lines)[0]
    got = lax.all_to_all(send.reshape(nd, nq, line), PLANE, 0, 0, tiled=True).reshape(nd * nq, line)
    part, half, rows0, rows_far, probs0 = call(
        functools.partial(down_kernel, nd, nq, nb, cap),
        [
            sds((slots, ff), F32),
            sds((slots, ff), BF),
            sds((slots, width), BF),
            sds((slots, width), BF),
            sds((slots, 1), F32),
        ],
        3,
        2 * product,
        slots * ff * 6,
    )(me, got, w_down, w_far)
    half = half.reshape(n_x, slots // n_x, ff)
    part = part.reshape(n_x, slots // n_x, ff)
    others = lax.all_to_all(half, "x", 0, 0, tiled=True)
    mine = lax.axis_index("x").astype(jnp.int32).reshape(1)
    piece = (slots // n_x, ff)
    eighth = call(
        sum_kernel, [sds(piece, BF)], 2, 0, slots * ff * 6
    )(mine, part, others)[0]
    other = lax.ppermute(eighth, "zh", SWAP)

    probs_later, _ = lax.optimization_barrier((probs0, eighth))
    f_gate, f_up, hidden = call(
        act_kernel, [sds((slots, ff), F32)] * 3, 3, slots * ff * 20, slots * ff * 16
    )(me, gate_pre[:, 0], up_pre[:, 0], probs_later)

    other, f_gate, f_up, hidden = lax.optimization_barrier((other, f_gate, f_up, hidden))
    u = call(
        pair_kernel, [sds((n_x,) + piece, BF)], 2, 0, slots * ff * 2, has_me=False
    )(eighth, other)[0]
    u0 = lax.all_to_all(u, "x", 0, 0, tiled=True).reshape(slots, ff)
    grads0, back = call(
        functools.partial(slot_kernel, nd, nq, nb, cap),
        [sds((2, slots, ff), BF), sds((nd * nq, line), BF)],
        8,
        4 * product,
        slots * ff * 24,
    )(me, u0, f_gate, f_up, hidden, w_gate, w_up, wg_far, wu_far)
    home = lax.all_to_all(back.reshape(nd, nq, line), PLANE, 0, 0, tiled=True)
    part = call(
        functools.partial(unpack_kernel, dims),
        [sds((nq * toks, wide), BF)],
        2,
        product // 4,
        nd * nq * line * 2,
    )(first, lines, home.reshape(nd * nq, line))[0]
    part, grads_now, rows_far, probs_now = lax.optimization_barrier(
        (part, grads0, rows_far, probs0)
    )
    grads1 = lax.ppermute(grads_now, "core", SWAP)
    rows1 = lax.ppermute(rows_far, "core", SWAP)
    probs1 = lax.ppermute(probs_now, "core", SWAP)
    grad_down = call(
        down_grad_kernel, [sds((ff, width), BF)], 6, 2 * product, slots * ff * 12
    )(me, gate_pre[:, 0], up_pre[:, 0], probs0, probs1, rows0, rows1)[0]
    part = lax.all_to_all(part.reshape(nq, toks, wide), ("core", "za"), 0, 0, tiled=True)
    grad_gate, grad_up = call(
        weight_kernel, [sds((width, ff), BF)] * 2, 3, 4 * product, slots * ff * 12
    )(me, saved_inputs[:, 0], grads0, grads1)
    in_grad, prob_grad = call(
        total_kernel,
        [sds((mb, toks, width), BF), sds((mb, top, toks), BF)],
        1,
        0,
        toks * width * 20,
        has_me=False,
    )(part)
    prob_grad = jnp.swapaxes(prob_grad, 1, 2)
    return in_grad, prob_grad, grad_gate[None], grad_up[None], grad_down[None]


def solution(mesh):
    n_dp, n_ex = mesh.devices.shape
    n_a = 4 if n_ex >= 64 else 2
    fine = Mesh(
        mesh.devices.reshape(2, n_dp // 4, 2, n_a, n_ex // (4 * n_a), 4),
        ("zh", "x", "core", "za", "zb", "y"),
    )
    specs = (
        P(None, EX, DP),
        P(None, EX, None),
        P(None, EX, None),
        P(None, EX, None, DP),
        P(None, EX, None, None),
        P(None, EX, None, None),
        P(EX, DP, None),
        P(EX, DP, None),
        P(EX, None, DP),
    )
    return jax.shard_map(
        local,
        mesh=fine,
        in_specs=specs,
        out_specs=(specs[0], specs[1], specs[6], specs[7], specs[8]),
        check_vma=False,
    )
```

```python
import functools

import jax
import jax.numpy as jnp
from jax import lax
from jax.experimental import pallas as pl
from jax.experimental.pallas import tpu as pltpu
from jax.sharding import Mesh
from jax.sharding import PartitionSpec as P

BF = jnp.bfloat16
F32 = jnp.float32
DP = ("zh", "x", "core")
EX = ("za", "zb", "y")
PLANE = ("zb", "y")
PAD = 128
SWAP = [(0, 1), (1, 0)]
VMEM = pl.BlockSpec(memory_space=pltpu.VMEM)
SMEM = pl.BlockSpec(memory_space=pltpu.SMEM)


def dot(a, b, ca, cb):
    return lax.dot_general(a, b, (((ca,), (cb,)), ((), ())), preferred_element_type=F32)


def iota(shape, dim):
    return lax.broadcasted_iota(jnp.int32, shape, dim)


def call(body, outs, n_in, flops, bytes_moved, limit=24, has_me=True):
    first = [SMEM] if has_me else []
    return pl.pallas_call(
        body,
        out_shape=outs,
        in_specs=first + [VMEM] * n_in,
        out_specs=[VMEM] * len(outs),
        cost_estimate=pl.CostEstimate(flops=flops, bytes_accessed=bytes_moved, transcendentals=0),
        compiler_params=pltpu.CompilerParams(vmem_limit_bytes=limit << 20),
    )


def flat_kernel(ids_in, probs_in, rows_in, out, ids, probs, rows, sems):
    copies = [
        pltpu.make_async_copy(source, held, sems.at[i])
        for i, (source, held) in enumerate(((ids_in, ids), (probs_in, probs), (rows_in, rows)))
    ]
    for copy in copies:
        copy.start()
    for copy in copies:
        copy.wait()
    mb, toks, width = rows.shape
    top = ids.shape[1]
    peers = out.shape[0] // mb
    ahead = iota((top, PAD), 1) - iota((top, PAD), 0)
    for m in range(mb):
        tail = dot(ids[m].astype(F32).astype(BF), (ahead == 0).astype(F32).astype(BF), 0, 0)
        tail = tail + dot(probs[m], (ahead == top).astype(F32).astype(BF), 0, 0)
        for peer in range(m * peers, (m + 1) * peers):
            out[peer, :, :width] = rows[m]
            out[peer, :, width:] = tail.astype(BF)


def route_maps(names, first, size, nq, toks, cap):
    tokens, top = names.shape
    shape = (tokens, size)
    column = iota(shape, 1)
    expert = (first + lax.div(column, nq)).astype(F32)
    same = lax.div(iota(shape, 0), toks) == lax.rem(column, nq)
    picks = [jnp.where(same & (names[:, k : k + 1] == expert), 1.0, 0.0) for k in range(top)]
    hits = functools.reduce(jnp.add, picks)
    lower = jnp.where(iota((tokens, tokens), 0) > iota((tokens, tokens), 1), 1.0, 0.0)
    slot = dot(lower.astype(BF), hits.astype(BF), 1, 0)
    return picks, [jnp.where(slot == s, hits, 0.0) for s in range(cap)]


def pack_kernel(dims, first, lines, out):
    nd, nq, toks, top, cap, width = dims
    tail_in = lines[:, width:].astype(F32)
    picks, maps = route_maps(tail_in[:, :top], first[0], nd * nq, nq, toks, cap)
    grads = lines[:, :width]
    tokens = grads.shape[0]
    held = functools.reduce(
        jnp.add, [k * tail_in[:, top + i : top + i + 1] for i, k in enumerate(picks)]
    )
    tail = jnp.zeros((nd * nq, PAD), F32)
    for s, k in enumerate(maps):
        out[:, s * width : (s + 1) * width] = dot(k.astype(BF), grads, 0, 0).astype(BF)
        lane = jnp.where(iota((tokens, PAD), 1) == s, 1.0, 0.0).astype(BF)
        tail = tail + dot((k * held).astype(BF), lane, 0, 0)
    out[:, cap * width :] = tail.astype(BF)


def unpack_kernel(dims, first, lines, home, out):
    nd, nq, toks, top, cap, width = dims
    names = lines[:, width:].astype(F32)[:, :top]
    picks, maps = route_maps(names, first[0], nd * nq, nq, toks, cap)
    tokens = names.shape[0]
    total = jnp.zeros((tokens, width), F32)
    held = jnp.zeros((tokens, nd * nq), F32)
    tail = home[:, cap * width :]
    for s, k in enumerate(maps):
        total = total + dot(k.astype(BF), home[:, s * width : (s + 1) * width], 1, 0)
        lane = jnp.where(iota((tokens, PAD), 1) == s, 1.0, 0.0).astype(BF)
        held = held + k * dot(lane, tail, 1, 1)
    out[:, :width] = total.astype(BF)
    lane = iota((tokens, PAD), 1)
    picked = jnp.zeros((tokens, PAD), F32)
    for i, k in enumerate(picks):
        picked = jnp.where(lane == i, jnp.sum(k * held, axis=1, keepdims=True), picked)
    out[:, width:] = picked.astype(BF)


def total_kernel(parts, in_grad, prob_grad):
    mb, toks, width = in_grad.shape
    top = prob_grad.shape[1]
    n = parts.shape[0] // mb
    column = (iota((top, PAD), 1) == iota((top, PAD), 0)).astype(F32).astype(BF)
    for m in range(mb):
        total = functools.reduce(
            jnp.add, [parts[i].astype(F32) for i in range(m * n, (m + 1) * n)]
        )
        in_grad[m] = total[:, :width].astype(BF)
        prob_grad[m] = dot(column, total[:, width:].astype(BF), 1, 1).astype(BF)


def first_row(shape, nd, nq, mb, cap):
    column = iota(shape, 1)
    return (lax.rem(lax.rem(column, nq), nq // mb) * nd + lax.div(column, nq)) * cap


def spread(nd, nq, mb, cap, m, s=None):
    rows = (nd * nq // mb) * cap
    shape = (rows, nd * nq)
    ahead = iota(shape, 0) - first_row(shape, nd, nq, mb, cap)
    here = (ahead >= 0) & (ahead < cap) if s is None else ahead == s
    here = here & (lax.div(lax.rem(iota(shape, 1), nq), nq // mb) == m)
    return jnp.where(here, 1.0, 0.0).astype(BF)


def down_kernel(nd, nq, nb, cap, me, got, w_mine, w_other, part, half, mine, other, probs):
    slots, width = mine.shape
    blocks = []
    for d in range(nb):
        total = jnp.zeros((slots, width), F32)
        for s in range(cap):
            total = total + dot(
                spread(nd, nq, nb, cap, d, s), got[:, s * width : (s + 1) * width], 1, 0
            )
        blocks.append(total)
    own = jnp.where(me[0] == 0, blocks[0], blocks[1]).astype(BF)
    far = jnp.where(me[0] == 0, blocks[1], blocks[0]).astype(BF)
    mine[...] = own
    other[...] = far
    total = dot(own, w_mine[...], 1, 1) + dot(far, w_other[...], 1, 1)
    part[...] = total
    half[...] = total.astype(BF)
    tail = dot(spread(nd, nq, nb, cap, 0), got[:, cap * width :], 1, 0)
    shape = (slots, PAD)
    probs[...] = jnp.sum(
        jnp.where(iota(shape, 1) == lax.rem(iota(shape, 0), cap), tail, 0.0), axis=1, keepdims=True
    )


def sum_kernel(mine, own, others, out):
    n = others.shape[0]
    total = functools.reduce(
        jnp.add, [jnp.where(mine[0] == i, own[i], others[i].astype(F32)) for i in range(n)]
    )
    out[...] = total.astype(BF)


def pair_kernel(first, second, out):
    total = (first[...].astype(F32) + second[...].astype(F32)).astype(BF)
    for i in range(out.shape[0]):
        out[i] = total


def act_kernel(me, gate, up, probs, f_gate, f_up, hidden):
    gate_f = gate[me[0]].astype(F32)
    up_f = up[me[0]].astype(F32)
    p = probs[...]
    sig = 1.0 / (1.0 + jnp.exp(-gate_f))
    act = gate_f * sig
    f_gate[...] = p * up_f * (sig * (1.0 + gate_f * (1.0 - sig)))
    f_up[...] = p * act
    hidden[...] = act * up_f


def down_grad_kernel(me, gate, up, probs0, probs1, rows0, rows1, grad):
    total = None
    for m, (probs, rows) in enumerate(((probs0, rows0), (probs1, rows1))):
        gate_f = gate[me[0] ^ m].astype(F32)
        act = gate_f * (1.0 / (1.0 + jnp.exp(-gate_f)))
        scaled = (probs[...] * (act * up[me[0] ^ m].astype(F32))).astype(BF)
        term = dot(scaled, rows[...], 0, 0)
        total = term if total is None else total + term
    grad[...] = total.astype(BF)


def slot_kernel(nd, nq, nb, cap, me, u_ref, f_gate, f_up, hidden, wg, wu, wg_far, wu_far, grads, out):
    u = u_ref[...].astype(F32)
    dg = (u * f_gate[...]).astype(BF)
    du = (u * f_up[...]).astype(BF)
    grads[0] = dg
    grads[1] = du
    own = dot(dg, wg[...], 1, 1) + dot(du, wu[...], 1, 1)
    far = dot(dg, wg_far[...], 1, 1) + dot(du, wu_far[...], 1, 1)
    blocks = [
        jnp.where(me[0] == 0, own, far).astype(BF),
        jnp.where(me[0] == 0, far, own).astype(BF),
    ]
    slots, width = blocks[0].shape
    for s in range(cap):
        lines = functools.reduce(
            jnp.add, [dot(spread(nd, nq, nb, cap, d, s), blocks[d], 0, 0) for d in range(nb)]
        )
        out[:, s * width : (s + 1) * width] = lines.astype(BF)
    slot_prob = jnp.sum(u * hidden[...], axis=1, keepdims=True)
    shape = (slots, PAD)
    tail = jnp.where(iota(shape, 1) == lax.rem(iota(shape, 0), cap), slot_prob, 0.0).astype(BF)
    tails = functools.reduce(
        jnp.add, [dot(spread(nd, nq, nb, cap, d), tail, 0, 0) for d in range(nb)]
    )
    out[:, cap * width :] = tails.astype(BF)


def weight_kernel(me, inputs, grads0, grads1, grad_gate, grad_up):
    first, second = inputs[me[0]], inputs[me[0] ^ 1]
    for i, out in enumerate((grad_gate, grad_up)):
        out[...] = (dot(first, grads0[i], 0, 0) + dot(second, grads1[i], 0, 0)).astype(BF)


def local(out_grad, expert_ids, probs, saved_inputs, gate_pre, up_pre, w_gate, w_up, w_down):
    sds = jax.ShapeDtypeStruct
    ne = lax.axis_size(EX)
    n_x = lax.axis_size("x")
    mb, toks, top = expert_ids.shape
    slots = saved_inputs.shape[2]
    cap = slots // ne
    width = out_grad.shape[2]
    ff = w_gate.shape[2]
    line = cap * width + PAD
    w_gate, w_up, w_down = w_gate[0], w_up[0], w_down[0]
    core = lax.axis_index("core")
    me = core.astype(jnp.int32).reshape(1)
    product = 2 * slots * width * ff

    n_a, nd = lax.axis_size("za"), lax.axis_size(PLANE)
    nb = mb
    nq = n_a * nb
    dims = (nd, nq, toks, top, cap, width)
    wide = width + PAD
    first = (lax.axis_index("za").astype(jnp.int32) * nd).reshape(1)

    hbm = pl.BlockSpec(memory_space=pltpu.HBM)
    flat = pl.pallas_call(
        flat_kernel,
        out_shape=sds((nq, toks, wide), BF),
        in_specs=[hbm, hbm, hbm],
        out_specs=VMEM,
        scratch_shapes=[
            pltpu.VMEM((mb, top, toks), jnp.int32),
            pltpu.VMEM((mb, top, toks), BF),
            pltpu.VMEM((mb, toks, width), BF),
            pltpu.SemaphoreType.DMA((3,)),
        ],
        compiler_params=pltpu.CompilerParams(vmem_limit_bytes=56 << 20),
    )(jnp.swapaxes(expert_ids, 1, 2), jnp.swapaxes(probs, 1, 2), out_grad)
    flat, *sent = lax.optimization_barrier((flat, w_down, w_gate, w_up))
    w_far, wg_far, wu_far = [lax.ppermute(w, "core", SWAP) for w in sent]
    lines = lax.all_to_all(flat, ("core", "za"), 0, 0, tiled=True).reshape(nq * toks, wide)
    lines, w_far, wg_far, wu_far = lax.optimization_barrier((lines, w_far, wg_far, wu_far))
    send = call(
        functools.partial(pack_kernel, dims), [sds((nd * nq, line), BF)], 1, 16 * product, nd * nq * line * 64
    )(first, lines)[0]
    got = lax.all_to_all(send.reshape(nd, nq, line), PLANE, 0, 0, tiled=True).reshape(nd * nq, line)
    part, half, rows0, rows_far, probs0 = call(
        functools.partial(down_kernel, nd, nq, nb, cap),
        [
            sds((slots, ff), F32),
            sds((slots, ff), BF),
            sds((slots, width), BF),
            sds((slots, width), BF),
            sds((slots, 1), F32),
        ],
        3,
        2 * product,
        slots * ff * 6,
    )(me, got, w_down, w_far)
    half = half.reshape(n_x, slots // n_x, ff)
    part = part.reshape(n_x, slots // n_x, ff)
    others = lax.all_to_all(half, "x", 0, 0, tiled=True)
    mine = lax.axis_index("x").astype(jnp.int32).reshape(1)
    piece = (slots // n_x, ff)
    eighth = call(
        sum_kernel, [sds(piece, BF)], 2, 0, slots * ff * 6
    )(mine, part, others)[0]
    other = lax.ppermute(eighth, "zh", SWAP)

    probs_later, _ = lax.optimization_barrier((probs0, eighth))
    f_gate, f_up, hidden = call(
        act_kernel, [sds((slots, ff), F32)] * 3, 3, slots * ff * 20, slots * ff * 16
    )(me, gate_pre[:, 0], up_pre[:, 0], probs_later)

    other, f_gate, f_up, hidden = lax.optimization_barrier((other, f_gate, f_up, hidden))
    u = call(
        pair_kernel, [sds((n_x,) + piece, BF)], 2, 0, slots * ff * 2, has_me=False
    )(eighth, other)[0]
    u0 = lax.all_to_all(u, "x", 0, 0, tiled=True).reshape(slots, ff)
    grads0, back = call(
        functools.partial(slot_kernel, nd, nq, nb, cap),
        [sds((2, slots, ff), BF), sds((nd * nq, line), BF)],
        8,
        4 * product,
        slots * ff * 24,
    )(me, u0, f_gate, f_up, hidden, w_gate, w_up, wg_far, wu_far)
    home = lax.all_to_all(back.reshape(nd, nq, line), PLANE, 0, 0, tiled=True)
    part = call(
        functools.partial(unpack_kernel, dims),
        [sds((nq * toks, wide), BF)],
        2,
        product // 4,
        nd * nq * line * 2,
    )(first, lines, home.reshape(nd * nq, line))[0]
    part, rows_far, probs_now = lax.optimization_barrier((part, rows_far, probs0))
    rows1 = lax.ppermute(rows_far, "core", SWAP)
    probs1 = lax.ppermute(probs_now, "core", SWAP)
    grads_now, rows1 = lax.optimization_barrier((grads0, rows1))
    grads1 = lax.ppermute(grads_now, "core", SWAP)
    grad_down = call(
        down_grad_kernel, [sds((ff, width), BF)], 6, 2 * product, slots * ff * 12
    )(me, gate_pre[:, 0], up_pre[:, 0], probs0, probs1, rows0, rows1)[0]
    part = lax.all_to_all(part.reshape(nq, toks, wide), ("core", "za"), 0, 0, tiled=True)
    grad_gate, grad_up = call(
        weight_kernel, [sds((width, ff), BF)] * 2, 3, 4 * product, slots * ff * 12
    )(me, saved_inputs[:, 0], grads0, grads1)
    part, grad_gate, grad_up, grad_down = lax.optimization_barrier(
        (part, grad_gate, grad_up, grad_down)
    )
    in_grad, prob_grad = call(
        total_kernel,
        [sds((mb, toks, width), BF), sds((mb, top, toks), BF)],
        1,
        0,
        toks * width * 20,
        has_me=False,
    )(part)
    prob_grad = jnp.swapaxes(prob_grad, 1, 2)
    return in_grad, prob_grad, grad_gate[None], grad_up[None], grad_down[None]


def solution(mesh):
    n_dp, n_ex = mesh.devices.shape
    n_a = 4 if n_ex >= 64 else 2
    fine = Mesh(
        mesh.devices.reshape(2, n_dp // 4, 2, n_a, n_ex // (4 * n_a), 4),
        ("zh", "x", "core", "za", "zb", "y"),
    )
    specs = (
        P(None, EX, DP),
        P(None, EX, None),
        P(None, EX, None),
        P(None, EX, None, DP),
        P(None, EX, None, None),
        P(None, EX, None, None),
        P(EX, DP, None),
        P(EX, DP, None),
        P(EX, None, DP),
    )
    return jax.shard_map(
        local,
        mesh=fine,
        in_specs=specs,
        out_specs=(specs[0], specs[1], specs[6], specs[7], specs[8]),
        check_vma=False,
    )
```
